32 devices in a mesh: layer: 8 (over z, core), dp: 2 (over y), mp: 2 (over x).
Axes of the slice: x: 2, y: 2, z: 4, core: 2. Of those that a mesh axis runs over, the one named last changes fastest.
Arguments:
- states: bfloat16 [32, 256, 1024], P('layer', 'dp'), may hold values from -6 to 6
- weights: bfloat16 [32, 1024, 1024], P('layer', 'dp', 'mp'), may hold values from -0.1875 to 0.1875
- guess_points: bfloat16 [8, 256, 1024], P('layer', 'dp'), may hold values from -2 to 2
- cotangent: bfloat16 [256, 1024], P('dp'), may hold values from -6 to 6
Outputs:
- adjoint: bfloat16 [32, 256, 1024], P('layer', 'dp', 'mp')
- weight_grads: float32 [32, 1024, 1024], P('layer', 'dp', 'mp')
The draws below stay inside these ranges and needn't reach their ends.
All inputs are finite; a program needn't handle non-finite values.
Results may differ from the reference program's by a relative error of at most 0.03.
Values may be sent and summed in bfloat16 or wider, within the bound.
A program may use at most 64 MiB of HBM per device.

```python
import jax
import jax.numpy as jnp
from jax import lax

D = 1024
ROWS_DEV = 128
LAYERS = 32
COARSE = 8
ROWS = 256


def level_of(own_key, shape, shards, least, top_value):
    loudness, own = 1.0, jax.random.fold_in(own_key, 6)
    for dim, parts in shards:
        draws = jnp.exp(jax.random.uniform(jax.random.fold_in(own, dim), (parts,), jnp.float32, least / len(shards), top_value / len(shards)))
        loudness = loudness * jnp.repeat(draws, shape[dim] // parts).reshape([-1 if axis == dim else 1 for axis in range(len(shape))])
    return loudness


def scatter_about(stream_key, extent, deviation, most, split=(), dtype=jnp.bfloat16):
    entries = deviation * jax.random.normal(stream_key, extent, jnp.float32)
    if split:
        entries = entries * level_of(stream_key, extent, split, -0.22, 0.18)
    return jnp.clip(entries, -most, most).astype(dtype)


def setup_inputs(seed: int = 0) -> dict:
    arg_keys = jax.random.split(jax.random.key(seed), 5)
    return {
        "states": scatter_about(arg_keys[0], (LAYERS, ROWS, D), 1.0, 6.0, ((0, 8), (1, 2))),
        "weights": scatter_about(arg_keys[1], (LAYERS, D, D), D ** -0.5, 0.1875, ((0, 8), (1, 2), (2, 2))),
        "guess_points": scatter_about(arg_keys[2], (COARSE, ROWS, D), 0.3, 2.0, ((0, 8), (1, 2))),
        "cotangent": scatter_about(arg_keys[3], (ROWS, D), 1.0, 6.0, ((0, 2),)),
    }


step_size = 0.1


def slope_of(inputs, weight_block):
    tangent = jnp.tanh(jnp.dot(inputs, weight_block, preferred_element_type=jnp.float32))
    return 1.0 - tangent * tangent


def apply_step(upper_adj, slope, weight_block, coefficient):
    scaled_rows = (upper_adj * slope).astype(jnp.bfloat16)
    product = jnp.dot(scaled_rows, weight_block.T, preferred_element_type=jnp.float32)
    return upper_adj + coefficient * product, scaled_rows


def reference(states, weights, guess_points, cotangent):
    layer_total = states.shape[0]
    point_total = guess_points.shape[0]
    factor = layer_total // point_total
    model_width = states.shape[2]
    terminal = cotangent.astype(jnp.float32)
    slopes = [None] * layer_total
    residuals = [None] * point_total
    upper_adj = terminal
    for layer_id in range(layer_total - 1, -1, -1):
        slopes[layer_id] = slope_of(states[layer_id], weights[layer_id])
        relaxed, unused = apply_step(upper_adj, slopes[layer_id], weights[layer_id], step_size)
        if layer_id % factor == 0:
            base_point = guess_points[layer_id // factor].astype(jnp.float32)
            residuals[layer_id // factor] = relaxed - base_point
            upper_adj = base_point
        else:
            upper_adj = relaxed
    errors = [None] * point_total
    carried = jnp.zeros_like(terminal)
    for point_id in range(point_total - 1, -1, -1):
        layer_id = point_id * factor
        stepped, unused = apply_step(carried, slopes[layer_id], weights[layer_id], factor * step_size)
        errors[point_id] = (stepped + residuals[point_id]).astype(jnp.bfloat16)
        carried = lax.optimization_barrier(errors[point_id]).astype(jnp.float32)
    adjoints = [None] * layer_total
    gradients = [None] * layer_total
    block_count = states.shape[1] // ROWS_DEV
    upper_adj = terminal
    for layer_id in range(layer_total - 1, -1, -1):
        current, scaled_rows = apply_step(upper_adj, slopes[layer_id], weights[layer_id], step_size)
        if layer_id % factor == 0:
            point_id = layer_id // factor
            current = guess_points[point_id].astype(jnp.float32) + errors[point_id].astype(jnp.float32)
        blocks_in = states[layer_id].reshape(block_count, ROWS_DEV, model_width).astype(jnp.float32)
        blocks_scaled = scaled_rows.reshape(block_count, ROWS_DEV, model_width).astype(jnp.float32)
        partial_terms = jnp.einsum("brd,brh->bdh", blocks_in, blocks_scaled).astype(jnp.bfloat16)
        partial_terms = lax.optimization_barrier(partial_terms).astype(jnp.float32)
        gradients[layer_id] = step_size * jnp.sum(partial_terms, axis=0)
        adjoints[layer_id] = current.astype(jnp.bfloat16)
        upper_adj = current
    return jnp.stack(adjoints), jnp.stack(gradients)
```

```python
import functools

import jax
import jax.numpy as jnp
from jax import lax
from jax.experimental import pallas as pl
from jax.experimental.pallas import tpu as pltpu
from jax.sharding import PartitionSpec as P

step_size = 0.1
f32, bf16 = jnp.float32, jnp.bfloat16
MESH = pl.DeviceIdType.MESH


def back_product(scaled_rows, weight_block):
    return lax.dot_general(
        scaled_rows, weight_block, (((1,), (1,)), ((), ())), preferred_element_type=f32
    )


def slope_of(inputs, weight_block):
    tangent = jnp.tanh(jnp.dot(inputs, weight_block, preferred_element_type=f32))
    return 1.0 - tangent * tangent


def cycle(
    slab_count, dp_count, layers,
    states, weights, guess, cotangent, adjoint, grads,
    gw, cw, npt, slopes, cslopes, vbuf, sbuf, terminal,
    exs, exr, r0s, r0r, resid, inc, oinc, ebuf, oe, sg, stg, stt,
    wsend, wrecv, csend, crecv, lsem, ssend, srecv, gsend, grecv,
    xsend, xrecv, nsend, nrecv, hsend, hrecv,
):
    slab, mine, j = lax.axis_index("layer"), lax.axis_index("dp"), lax.axis_index("mp")
    o = 1 - j
    rows, width = states.shape[1], states.shape[2]
    blk, cols = weights.shape[1], weights.shape[2]
    half = rows // 2
    peers = range(1, dp_count)
    to_peer = [lax.rem(mine + d, dp_count) for d in peers]
    from_peer = [lax.rem(mine + dp_count - d, dp_count) for d in peers]
    not_top, not_low = slab < slab_count - 1, slab > 0
    own_in = pl.ds(pl.multiple_of(mine * blk, blk), blk)
    own_rows = pl.ds(pl.multiple_of(mine * rows, rows), rows)
    half_j = pl.ds(pl.multiple_of(j * half, half), half)
    half_o = pl.ds(pl.multiple_of(o * half, half), half)
    cols_j = pl.ds(pl.multiple_of(j * cols, cols), cols)
    cols_o = pl.ds(pl.multiple_of(o * cols, cols), cols)

    def remote(src, dst, send, recv, device):
        return pltpu.make_async_remote_copy(
            src_ref=src, dst_ref=dst, send_sem=send, recv_sem=recv,
            device_id=device, device_id_type=MESH,
        )

    barrier = pltpu.get_barrier_semaphore()

    def greet(device):
        pl.semaphore_signal(barrier, inc=1, device_id=device, device_id_type=MESH)

    for peer in to_peer:
        greet({"dp": peer})
    greet({"mp": o})

    @pl.when(not_top)
    def _():
        greet({"layer": slab + 1})

    @pl.when(not_low)
    def _():
        greet({"layer": slab - 1})

    pl.semaphore_wait(
        barrier, dp_count + not_top.astype(jnp.int32) + not_low.astype(jnp.int32)
    )

    def home(layer):
        return cw.at[j] if layer == 0 else gw.at[layer - 1]

    partner = {"mp": o}
    point_copy = remote(guess.at[0, :, cols_j], npt, nsend.at[0], nrecv.at[0], {"layer": slab - 1})

    @pl.when(not_low)
    def _():
        point_copy.start()

    w_copies, local_copies = {}, {}
    c_copies = [remote(weights.at[0], cw.at[j, own_in], csend.at[0], crecv.at[0], partner)]
    c_copies[0].start()
    order = [0] + list(range(layers - 1, 0, -1))
    for layer in order:
        for d in peers:
            w_copies[layer, d] = remote(
                weights.at[layer], home(layer).at[own_in],
                wsend.at[layer, d - 1], wrecv.at[layer, d - 1], {"dp": to_peer[d - 1]},
            )
            w_copies[layer, d].start()
    for layer in order:
        local_copies[layer] = pltpu.make_async_copy(
            weights.at[layer], home(layer).at[own_in], lsem.at[layer]
        )
        local_copies[layer].start()

    @pl.when(not_top)
    def _():
        point_copy.wait_recv()
        terminal[...] = npt[...].astype(f32)

    @pl.when(jnp.logical_not(not_top))
    def _():
        terminal[...] = cotangent[:, cols_j].astype(f32)

    local_copies[0].wait()
    for d in peers:
        w_copies[0, d].wait_recv()
        block = pl.ds(pl.multiple_of(from_peer[d - 1] * blk, blk), blk)
        c_copies.append(
            remote(cw.at[j, block], cw.at[j, block], csend.at[d], crecv.at[d], partner)
        )
        c_copies[d].start()
    slopes[0] = slope_of(states[0], cw[j])

    pending = []

    def exchange_step(slot, layer, v, s, between=None):
        w = home(layer)
        exs[slot] = (step_size * back_product(s, w[cols_o, :])).astype(bf16)
        copy = remote(exs.at[slot], exr.at[slot], xsend.at[slot], xrecv.at[slot], partner)
        copy.start()
        pending.append(copy)
        v = v + step_size * back_product(s, w[cols_j, :])
        if between is not None:
            between()
        copy.wait_recv()
        return v + exr[slot].astype(f32)

    v = terminal[...]
    slot = 0
    for layer in range(layers - 1, 0, -1):
        local_copies[layer].wait()
        for d in peers:
            w_copies[layer, d].wait_recv()
        slopes[layer] = slope_of(states[layer], gw[layer - 1])
        s = (v * slopes[layer]).astype(bf16)
        v = exchange_step(slot, layer, v, s)
        slot += 1
    vbuf[...] = v
    sbuf[...] = (v * slopes[0]).astype(bf16)
    s_far = sbuf[half_o, :]
    for c in range(2):
        far = step_size * back_product(s_far, cw[j, c * cols:(c + 1) * cols, :])
        r0s[c] = (far + jnp.where(j == c, vbuf[half_o, :], 0.0)).astype(bf16)
    r0_copy = remote(r0s, r0r, xsend.at[slot], xrecv.at[slot], partner)
    r0_copy.start()
    pending.append(r0_copy)
    slot_r0 = slot

    s_copies = []
    for d in peers:
        block = pl.ds(pl.multiple_of(to_peer[d - 1] * blk, blk), blk)
        s_copies.append(
            remote(states.at[:, :, block], stg.at[:, own_rows, :], ssend.at[d - 1],
                   srecv.at[d - 1], {"dp": to_peer[d - 1]})
        )
        s_copies[-1].start()

    s_near = sbuf[half_j, :]
    for c in range(2):
        near = step_size * back_product(s_near, cw[j, c * cols:(c + 1) * cols, :])
        near = near + jnp.where(j == c, vbuf[half_j, :], 0.0)
        resid[c] = near - guess[0, half_j, c * cols:(c + 1) * cols].astype(f32)
    for c_copy in c_copies:
        c_copy.wait_recv()
    cslopes[j] = slopes[0, half_j, :]
    cslopes[o] = slope_of(states[0, half_j, :], cw[o])
    r0_copy.wait_recv()
    for c in range(2):
        resid[c] = resid[c] + r0r[c].astype(f32)

    for layer in range(layers):
        stg[layer, own_rows, :] = states[layer, :, own_in]
    for s_copy in s_copies:
        s_copy.wait_recv()
    for layer in range(layers):
        stt[layer] = stg[layer].T

    chain = [
        remote(ebuf.at[c], inc.at[c], hsend.at[c], hrecv.at[c], {"layer": slab - 1})
        for c in range(2)
    ]

    @pl.when(not_top)
    def _():
        for c in range(2):
            chain[c].wait_recv()

    @pl.when(jnp.logical_not(not_top))
    def _():
        inc[...] = jnp.zeros_like(inc)

    pass_on = remote(inc.at[o], oinc, xsend.at[slot + 1], xrecv.at[slot + 1], partner)
    pass_on.start()
    pending.append(pass_on)
    carried = [inc[c].astype(f32) for c in range(2)]
    coarse_scaled = [(carried[c] * cslopes[c]).astype(bf16) for c in range(2)]
    for c in range(2):
        block = slice(c * cols, (c + 1) * cols)
        product = back_product(coarse_scaled[0], cw[0, block, :]) + back_product(
            coarse_scaled[1], cw[1, block, :]
        )
        ebuf[c] = (carried[c] + layers * step_size * product + resid[c]).astype(bf16)

        @pl.when(not_low)
        def _():
            chain[c].start()

    e_copy = remote(ebuf.at[o], oe, xsend.at[slot + 2], xrecv.at[slot + 2], partner)
    e_copy.start()
    pending.append(e_copy)

    vbuf[half_j, :] = terminal[half_j, :] + inc[j].astype(f32)
    pass_on.wait_recv()
    vbuf[half_o, :] = terminal[half_o, :] + oinc[...].astype(f32)
    v = vbuf[...]
    g_copies = {}

    def spread(layer, s):
        sg[layer, own_rows, :] = s
        for d in peers:
            g_copies[layer, d] = remote(
                sg.at[layer, own_rows], sg.at[layer, own_rows],
                gsend.at[layer, d - 1], grecv.at[layer, d - 1], {"dp": to_peer[d - 1]},
            )
            g_copies[layer, d].start()

    def gradient(layer):
        for d in peers:
            g_copies[layer, d].wait_recv()
        grads[layer] = step_size * jnp.dot(stt[layer], sg[layer], preferred_element_type=f32)

    slot = slot_r0 + 3
    for layer in range(layers - 1, 0, -1):
        s = (v * slopes[layer]).astype(bf16)
        spread(layer, s)
        between = functools.partial(gradient, layer + 1) if layer < layers - 1 else None
        v = exchange_step(slot, layer, v, s, between)
        slot += 1
        adjoint[layer] = v.astype(bf16)
    spread(0, (v * slopes[0]).astype(bf16))
    if layers > 1:
        gradient(1)
    e_copy.wait_recv()
    adjoint[0, half_j, :] = (guess[0, half_j, cols_j].astype(f32) + ebuf[j].astype(f32)).astype(bf16)
    adjoint[0, half_o, :] = (guess[0, half_o, cols_j].astype(f32) + oe[...].astype(f32)).astype(bf16)
    gradient(0)

    for copy in pending + c_copies + s_copies + list(w_copies.values()) + list(g_copies.values()):
        copy.wait_send()

    @pl.when(not_low)
    def _():
        point_copy.wait_send()
        for c in range(2):
            chain[c].wait_send()


def solution(mesh):
    slab_count, dp_count, mp_count = (mesh.shape[a] for a in ("layer", "dp", "mp"))
    assert mp_count == 2

    def body(states, weights, guess_points, cotangent):
        layers, rows, width = states.shape
        blk, cols = weights.shape[1:]
        assert guess_points.shape[0] == 1
        half = rows // 2
        slots = 2 * layers + 2
        all_rows = rows * dp_count
        dma = pltpu.SemaphoreType.DMA
        vmem = pl.BlockSpec(memory_space=pltpu.VMEM)
        return pl.pallas_call(
            functools.partial(cycle, slab_count, dp_count, layers),
            out_shape=(
                jax.ShapeDtypeStruct((layers, rows, cols), bf16),
                jax.ShapeDtypeStruct((layers, blk, cols), f32),
            ),
            in_specs=[vmem] * 4,
            out_specs=(vmem, vmem),
            scratch_shapes=[
                pltpu.VMEM((layers - 1, width, cols), bf16),
                pltpu.VMEM((2, width, cols), bf16),
                pltpu.VMEM((rows, cols), bf16),
                pltpu.VMEM((layers, rows, cols), f32),
                pltpu.VMEM((2, half, cols), f32),
                pltpu.VMEM((rows, cols), f32),
                pltpu.VMEM((rows, cols), bf16),
                pltpu.VMEM((rows, cols), f32),
                pltpu.VMEM((slots, rows, cols), bf16),
                pltpu.VMEM((slots, rows, cols), bf16),
                pltpu.VMEM((2, half, cols), bf16),
                pltpu.VMEM((2, half, cols), bf16),
                pltpu.VMEM((2, half, cols), f32),
                pltpu.VMEM((2, half, cols), bf16),
                pltpu.VMEM((half, cols), bf16),
                pltpu.VMEM((2, half, cols), bf16),
                pltpu.VMEM((half, cols), bf16),
                pltpu.VMEM((layers, all_rows, cols), bf16),
                pltpu.VMEM((layers, all_rows, blk), bf16),
                pltpu.VMEM((layers, blk, all_rows), bf16),
                dma((layers, dp_count - 1)), dma((layers, dp_count - 1)),
                dma((dp_count,)), dma((dp_count,)),
                dma((layers,)),
                dma((dp_count - 1,)), dma((dp_count - 1,)),
                dma((layers, dp_count - 1)), dma((layers, dp_count - 1)),
                dma((slots,)), dma((slots,)),
                dma((1,)), dma((1,)),
                dma((2,)), dma((2,)),
            ],
            compiler_params=pltpu.CompilerParams(
                collective_id=0, has_side_effects=True, vmem_limit_bytes=56 * 2**20
            ),
            cost_estimate=pl.CostEstimate(
                flops=12 * layers * rows * width * cols, bytes_accessed=2**23, transcendentals=0
            ),
        )(states, weights, guess_points, cotangent)

    return jax.shard_map(
        body,
        mesh=mesh,
        in_specs=(
            P("layer", "dp", None),
            P("layer", "dp", "mp"),
            P("layer", "dp", None),
            P("dp", None),
        ),
        out_specs=(P("layer", "dp", "mp"), P("layer", "dp", "mp")),
        check_vma=False,
    )
```

```python
import functools

import jax
import jax.numpy as jnp
from jax import lax
from jax.experimental import pallas as pl
from jax.experimental.pallas import tpu as pltpu
from jax.sharding import PartitionSpec as P

step_size = 0.1
f32, bf16 = jnp.float32, jnp.bfloat16
MESH = pl.DeviceIdType.MESH


def back_product(scaled_rows, weight_block):
    return lax.dot_general(
        scaled_rows, weight_block, (((1,), (1,)), ((), ())), preferred_element_type=f32
    )


def slope_of(inputs, weight_block):
    tangent = jnp.tanh(jnp.dot(inputs, weight_block, preferred_element_type=f32))
    return 1.0 - tangent * tangent


def cycle(
    slab_count, dp_count, layers,
    states_in, weights, guess, cotangent, adjoint, sg, stg,
    states, gw, cw, npt, slopes, cslopes, vbuf, sbuf, terminal,
    exs, exr, r0s, r0r, resid, inc, oinc, ebuf, oe, sown,
    wsend, wrecv, csend, crecv, lsem, osem, ssend, srecv, gsend, grecv,
    xsend, xrecv, nsend, nrecv, hsend, hrecv,
):
    slab, mine, j = lax.axis_index("layer"), lax.axis_index("dp"), lax.axis_index("mp")
    o = 1 - j
    rows, width = states.shape[1], states.shape[2]
    blk, cols = weights.shape[1], weights.shape[2]
    half = rows // 2
    peers = range(1, dp_count)
    to_peer = [lax.rem(mine + d, dp_count) for d in peers]
    from_peer = [lax.rem(mine + dp_count - d, dp_count) for d in peers]
    not_top, not_low = slab < slab_count - 1, slab > 0
    own_in = pl.ds(pl.multiple_of(mine * blk, blk), blk)
    own_rows = pl.ds(pl.multiple_of(mine * rows, rows), rows)
    half_j = pl.ds(pl.multiple_of(j * half, half), half)
    half_o = pl.ds(pl.multiple_of(o * half, half), half)
    cols_j = pl.ds(pl.multiple_of(j * cols, cols), cols)
    cols_o = pl.ds(pl.multiple_of(o * cols, cols), cols)

    def remote(src, dst, send, recv, device):
        return pltpu.make_async_remote_copy(
            src_ref=src, dst_ref=dst, send_sem=send, recv_sem=recv,
            device_id=device, device_id_type=MESH,
        )

    barrier = pltpu.get_barrier_semaphore()

    def greet(device):
        pl.semaphore_signal(barrier, inc=1, device_id=device, device_id_type=MESH)

    for peer in to_peer:
        greet({"dp": peer})
    greet({"mp": o})

    @pl.when(not_top)
    def _():
        greet({"layer": slab + 1})

    @pl.when(not_low)
    def _():
        greet({"layer": slab - 1})

    pl.semaphore_wait(
        barrier, dp_count + not_top.astype(jnp.int32) + not_low.astype(jnp.int32)
    )

    states_copy = pltpu.make_async_copy(states_in, states, osem.at[0])
    states_copy.start()

    def home(layer):
        return cw.at[j] if layer == 0 else gw.at[layer - 1]

    partner = {"mp": o}
    point_copy = remote(guess.at[0, :, cols_j], npt, nsend.at[0], nrecv.at[0], {"layer": slab - 1})

    @pl.when(not_low)
    def _():
        point_copy.start()

    w_copies, local_copies = {}, {}
    c_copies = [remote(weights.at[0], cw.at[j, own_in], csend.at[0], crecv.at[0], partner)]
    c_copies[0].start()
    order = [0] + list(range(layers - 1, 0, -1))
    for layer in order:
        for d in peers:
            w_copies[layer, d] = remote(
                weights.at[layer], home(layer).at[own_in],
                wsend.at[layer, d - 1], wrecv.at[layer, d - 1], {"dp": to_peer[d - 1]},
            )
            w_copies[layer, d].start()
    for layer in order:
        local_copies[layer] = pltpu.make_async_copy(
            weights.at[layer], home(layer).at[own_in], lsem.at[layer]
        )
        local_copies[layer].start()

    @pl.when(not_top)
    def _():
        point_copy.wait_recv()
        terminal[...] = npt[...].astype(f32)

    @pl.when(jnp.logical_not(not_top))
    def _():
        terminal[...] = cotangent[:, cols_j].astype(f32)

    local_copies[0].wait()
    for d in peers:
        w_copies[0, d].wait_recv()
        block = pl.ds(pl.multiple_of(from_peer[d - 1] * blk, blk), blk)
        c_copies.append(
            remote(cw.at[j, block], cw.at[j, block], csend.at[d], crecv.at[d], partner)
        )
        c_copies[d].start()
    states_copy.wait()
    slopes[0] = slope_of(states[0], cw[j])

    pending = []

    def exchange_step(slot, layer, v, s):
        w = home(layer)
        exs[slot] = (step_size * back_product(s, w[cols_o, :])).astype(bf16)
        copy = remote(exs.at[slot], exr.at[slot], xsend.at[slot], xrecv.at[slot], partner)
        copy.start()
        pending.append(copy)
        v = v + step_size * back_product(s, w[cols_j, :])
        copy.wait_recv()
        return v + exr[slot].astype(f32)

    v = terminal[...]
    slot = 0
    for layer in range(layers - 1, 0, -1):
        local_copies[layer].wait()
        for d in peers:
            w_copies[layer, d].wait_recv()
        slopes[layer] = slope_of(states[layer], gw[layer - 1])
        s = (v * slopes[layer]).astype(bf16)
        v = exchange_step(slot, layer, v, s)
        slot += 1
    vbuf[...] = v
    sbuf[...] = (v * slopes[0]).astype(bf16)
    s_far = sbuf[half_o, :]
    for c in range(2):
        far = step_size * back_product(s_far, cw[j, c * cols:(c + 1) * cols, :])
        r0s[c] = (far + jnp.where(j == c, vbuf[half_o, :], 0.0)).astype(bf16)
    r0_copy = remote(r0s, r0r, xsend.at[slot], xrecv.at[slot], partner)
    r0_copy.start()
    pending.append(r0_copy)
    slot_r0 = slot

    s_copies = []
    for d in peers:
        block = pl.ds(pl.multiple_of(to_peer[d - 1] * blk, blk), blk)
        s_copies.append(
            remote(states_in.at[:, :, block], stg.at[:, own_rows, :], ssend.at[d - 1],
                   srecv.at[d - 1], {"dp": to_peer[d - 1]})
        )
        s_copies[-1].start()

    own_states = pltpu.make_async_copy(
        states_in.at[:, :, own_in], stg.at[:, own_rows, :], osem.at[1]
    )
    own_states.start()

    s_near = sbuf[half_j, :]
    for c in range(2):
        near = step_size * back_product(s_near, cw[j, c * cols:(c + 1) * cols, :])
        near = near + jnp.where(j == c, vbuf[half_j, :], 0.0)
        resid[c] = near - guess[0, half_j, c * cols:(c + 1) * cols].astype(f32)
    for c_copy in c_copies:
        c_copy.wait_recv()
    cslopes[j] = slopes[0, half_j, :]
    cslopes[o] = slope_of(states[0, half_j, :], cw[o])
    r0_copy.wait_recv()
    for c in range(2):
        resid[c] = resid[c] + r0r[c].astype(f32)

    chain = [
        remote(ebuf.at[c], inc.at[c], hsend.at[c], hrecv.at[c], {"layer": slab - 1})
        for c in range(2)
    ]

    @pl.when(jnp.logical_not(not_top))
    def _():
        inc[...] = jnp.zeros_like(inc)

    carried, products = [], [0.0, 0.0]
    blocks = [slice(n * cols, (n + 1) * cols) for n in range(2)]

    def chain_out(n):
        total = carried[n] + layers * step_size * products[n] + resid[n]
        ebuf[n] = total.astype(bf16)

        @pl.when(not_low)
        def _():
            chain[n].start()

    for c in range(2):

        @pl.when(not_top)
        def _():
            chain[c].wait_recv()

        carried.append(inc[c].astype(f32))
        scaled_rows = (carried[c] * cslopes[c]).astype(bf16)
        for n in range(2):
            products[n] = products[n] + back_product(scaled_rows, cw[c, blocks[n], :])
            if c == 1:
                chain_out(n)
    pass_on = remote(inc.at[o], oinc, xsend.at[slot + 1], xrecv.at[slot + 1], partner)
    pass_on.start()
    pending.append(pass_on)

    e_copy = remote(ebuf.at[o], oe, xsend.at[slot + 2], xrecv.at[slot + 2], partner)
    e_copy.start()
    pending.append(e_copy)

    vbuf[half_j, :] = terminal[half_j, :] + inc[j].astype(f32)
    pass_on.wait_recv()
    vbuf[half_o, :] = terminal[half_o, :] + oinc[...].astype(f32)
    v = vbuf[...]
    g_copies = {}

    own_scaled = []

    def spread(layer, s):
        sown[layer] = s
        for d in peers:
            g_copies[layer, d] = remote(
                sown.at[layer], sg.at[layer, own_rows],
                gsend.at[layer, d - 1], grecv.at[layer, d - 1], {"dp": to_peer[d - 1]},
            )
            g_copies[layer, d].start()
        own_scaled.append(
            pltpu.make_async_copy(sown.at[layer], sg.at[layer, own_rows], osem.at[2 + layer])
        )
        own_scaled[-1].start()

    slot = slot_r0 + 3
    for layer in range(layers - 1, 0, -1):
        s = (v * slopes[layer]).astype(bf16)
        spread(layer, s)
        v = exchange_step(slot, layer, v, s)
        slot += 1
        adjoint[layer] = v.astype(bf16)
    spread(0, (v * slopes[0]).astype(bf16))
    e_copy.wait_recv()
    adjoint[0, half_j, :] = (guess[0, half_j, cols_j].astype(f32) + ebuf[j].astype(f32)).astype(bf16)
    adjoint[0, half_o, :] = (guess[0, half_o, cols_j].astype(f32) + oe[...].astype(f32)).astype(bf16)
    for copy in s_copies + list(g_copies.values()):
        copy.wait_recv()
    for copy in own_scaled + [own_states]:
        copy.wait()
    for copy in pending + c_copies + s_copies + list(w_copies.values()) + list(g_copies.values()):
        copy.wait_send()

    @pl.when(not_low)
    def _():
        point_copy.wait_send()
        for c in range(2):
            chain[c].wait_send()


def weight_gradients(inputs, scaled, adjoint_in, grads, adjoint):
    product = lax.dot_general(
        inputs[0], scaled[0], (((0,), (0,)), ((), ())), preferred_element_type=f32
    )
    grads[0] = step_size * product
    adjoint[...] = adjoint_in[...]


def solution(mesh):
    slab_count, dp_count, mp_count = (mesh.shape[a] for a in ("layer", "dp", "mp"))
    assert mp_count == 2

    def body(states, weights, guess_points, cotangent):
        layers, rows, width = states.shape
        blk, cols = weights.shape[1:]
        assert guess_points.shape[0] == 1
        half = rows // 2
        slots = 2 * layers + 2
        all_rows = rows * dp_count
        dma = pltpu.SemaphoreType.DMA
        vmem = pl.BlockSpec(memory_space=pltpu.VMEM)
        anywhere = pl.BlockSpec(memory_space=pl.ANY)
        adjoint, scaled, inputs = pl.pallas_call(
            functools.partial(cycle, slab_count, dp_count, layers),
            out_shape=(
                jax.ShapeDtypeStruct((layers, rows, cols), bf16),
                jax.ShapeDtypeStruct((layers, all_rows, cols), bf16),
                jax.ShapeDtypeStruct((layers, all_rows, blk), bf16),
            ),
            in_specs=[anywhere, anywhere, vmem, vmem],
            out_specs=(vmem, anywhere, anywhere),
            scratch_shapes=[
                pltpu.VMEM((layers, rows, width), bf16),
                pltpu.VMEM((layers - 1, width, cols), bf16),
                pltpu.VMEM((2, width, cols), bf16),
                pltpu.VMEM((rows, cols), bf16),
                pltpu.VMEM((layers, rows, cols), f32),
                pltpu.VMEM((2, half, cols), f32),
                pltpu.VMEM((rows, cols), f32),
                pltpu.VMEM((rows, cols), bf16),
                pltpu.VMEM((rows, cols), f32),
                pltpu.VMEM((slots, rows, cols), bf16),
                pltpu.VMEM((slots, rows, cols), bf16),
                pltpu.VMEM((2, half, cols), bf16),
                pltpu.VMEM((2, half, cols), bf16),
                pltpu.VMEM((2, half, cols), f32),
                pltpu.VMEM((2, half, cols), bf16),
                pltpu.VMEM((half, cols), bf16),
                pltpu.VMEM((2, half, cols), bf16),
                pltpu.VMEM((half, cols), bf16),
                pltpu.VMEM((layers, rows, cols), bf16),
                dma((layers, dp_count - 1)), dma((layers, dp_count - 1)),
                dma((dp_count,)), dma((dp_count,)),
                dma((layers,)), dma((layers + 2,)),
                dma((dp_count - 1,)), dma((dp_count - 1,)),
                dma((layers, dp_count - 1)), dma((layers, dp_count - 1)),
                dma((slots,)), dma((slots,)),
                dma((1,)), dma((1,)),
                dma((2,)), dma((2,)),
            ],
            compiler_params=pltpu.CompilerParams(
                collective_id=0, has_side_effects=True, vmem_limit_bytes=56 * 2**20
            ),
            cost_estimate=pl.CostEstimate(
                flops=12 * layers * rows * width * cols, bytes_accessed=2**23, transcendentals=0
            ),
        )(states, weights, guess_points, cotangent)

        def per_layer(*shape):
            return pl.BlockSpec((1, *shape), lambda layer: (layer, 0, 0))

        grads, adjoint = pl.pallas_call(
            weight_gradients,
            grid=(layers,),
            out_shape=(
                jax.ShapeDtypeStruct((layers, blk, cols), f32),
                jax.ShapeDtypeStruct((layers, rows, cols), bf16),
            ),
            in_specs=[per_layer(all_rows, blk), per_layer(all_rows, cols), per_layer(rows, cols)],
            out_specs=(per_layer(blk, cols), per_layer(rows, cols)),
            compiler_params=pltpu.CompilerParams(vmem_limit_bytes=32 * 2**20),
        )(inputs, scaled, adjoint)
        return adjoint, grads

    return jax.shard_map(
        body,
        mesh=mesh,
        in_specs=(
            P("layer", "dp", None),
            P("layer", "dp", "mp"),
            P("layer", "dp", None),
            P("dp", None),
        ),
        out_specs=(P("layer", "dp", "mp"), P("layer", "dp", "mp")),
        check_vma=False,
    )
```

```python
import functools

import jax
import jax.numpy as jnp
from jax import lax
from jax.experimental import pallas as pl
from jax.experimental.pallas import tpu as pltpu
from jax.sharding import PartitionSpec as P

step_size = 0.1
f32, bf16 = jnp.float32, jnp.bfloat16
MESH = pl.DeviceIdType.MESH


def back_product(scaled_rows, weight_block):
    return lax.dot_general(
        scaled_rows, weight_block, (((1,), (1,)), ((), ())), preferred_element_type=f32
    )


def slope_of(inputs, weight_block):
    tangent = jnp.tanh(jnp.dot(inputs, weight_block, preferred_element_type=f32))
    return 1.0 - tangent * tangent


def cycle(
    slab_count, dp_count, layers,
    states_in, weights, guess, cotangent, adjoint, sg, stg,
    states, gw, cw, npt, slopes, cslopes, vbuf, sbuf, terminal,
    exs, exr, r0s, r0r, resid, inc, oinc, ebuf, oe, sown,
    wsend, wrecv, csend, crecv, lsem, osem, ssend, srecv, gsend, grecv,
    xsend, xrecv, rsend, rrecv, psend, precv, nsend, nrecv, hsend, hrecv,
):
    slab, mine, j = lax.axis_index("layer"), lax.axis_index("dp"), lax.axis_index("mp")
    o = 1 - j
    rows, width = states.shape[1], states.shape[2]
    blk, cols = weights.shape[1], weights.shape[2]
    half = rows // 2
    peers = range(1, dp_count)
    to_peer = [lax.rem(mine + d, dp_count) for d in peers]
    from_peer = [lax.rem(mine + dp_count - d, dp_count) for d in peers]
    not_top, not_low = slab < slab_count - 1, slab > 0
    own_in = pl.ds(pl.multiple_of(mine * blk, blk), blk)
    own_rows = pl.ds(pl.multiple_of(mine * rows, rows), rows)
    half_j = pl.ds(pl.multiple_of(j * half, half), half)
    half_o = pl.ds(pl.multiple_of(o * half, half), half)
    cols_j = pl.ds(pl.multiple_of(j * cols, cols), cols)
    cols_o = pl.ds(pl.multiple_of(o * cols, cols), cols)

    def remote(src, dst, send, recv, device):
        return pltpu.make_async_remote_copy(
            src_ref=src, dst_ref=dst, send_sem=send, recv_sem=recv,
            device_id=device, device_id_type=MESH,
        )

    barrier = pltpu.get_barrier_semaphore()

    def greet(device):
        pl.semaphore_signal(barrier, inc=1, device_id=device, device_id_type=MESH)

    for peer in to_peer:
        greet({"dp": peer})
    greet({"mp": o})

    @pl.when(not_top)
    def _():
        greet({"layer": slab + 1})

    @pl.when(not_low)
    def _():
        greet({"layer": slab - 1})

    pl.semaphore_wait(
        barrier, dp_count + not_top.astype(jnp.int32) + not_low.astype(jnp.int32)
    )

    states_copy = pltpu.make_async_copy(states_in, states, osem.at[0])
    states_copy.start()

    def home(layer):
        return cw.at[j] if layer == 0 else gw.at[layer - 1]

    partner = {"mp": o}
    point_copy = remote(guess.at[0, :, cols_j], npt, nsend.at[0], nrecv.at[0], {"layer": slab - 1})

    @pl.when(not_low)
    def _():
        point_copy.start()

    w_copies, local_copies = {}, {}
    pieces = 4
    piece = blk // pieces

    def piece_of(owner, n):
        return pl.ds(pl.multiple_of(owner * blk + n * piece, piece), piece)

    c_copies = [remote(weights.at[0], cw.at[j, own_in], csend.at[0, 0], crecv.at[0, 0], partner)]
    c_copies[0].start()
    order = range(layers - 1, -1, -1)
    for layer in order:
        parts = pieces if layer == 0 else 1
        for n in range(parts):
            for d in peers:
                source = weights.at[layer, n * piece:(n + 1) * piece] if layer == 0 else weights.at[layer]
                target = cw.at[j, piece_of(mine, n)] if layer == 0 else home(layer).at[own_in]
                sem = pieces - 1 + layer if layer else n
                w_copies[layer, n, d] = remote(
                    source, target, wsend.at[sem, d - 1], wrecv.at[sem, d - 1],
                    {"dp": to_peer[d - 1]},
                )
                w_copies[layer, n, d].start()
    for layer in order:
        local_copies[layer] = pltpu.make_async_copy(
            weights.at[layer], home(layer).at[own_in], lsem.at[layer]
        )
        local_copies[layer].start()

    @pl.when(not_top)
    def _():
        point_copy.wait_recv()
        terminal[...] = npt[...].astype(f32)

    @pl.when(jnp.logical_not(not_top))
    def _():
        terminal[...] = cotangent[:, cols_j].astype(f32)

    pending = []
    span = [slice(0, half), slice(half, 2 * half)]

    def fine_half(slot, h, layer, scaled_rows):
        w = home(layer)
        exs[slot, h] = (step_size * back_product(scaled_rows, w[cols_o, :])).astype(bf16)
        copy = remote(
            exs.at[slot, h], exr.at[slot, h], xsend.at[slot, h], xrecv.at[slot, h], partner
        )
        copy.start()
        pending.append(copy)
        return copy, step_size * back_product(scaled_rows, w[cols_j, :])

    def arrived(value, copy, slot, h):
        if copy is None:
            return value
        copy.wait_recv()
        return value + exr[slot, h].astype(f32)

    v = [terminal[span[h], :] for h in range(2)]
    flying = [None, None]
    states_copy.wait()
    for slot, layer in enumerate(range(layers - 1, 0, -1)):
        local_copies[layer].wait()
        for d in peers:
            w_copies[layer, 0, d].wait_recv()
        slopes[layer] = slope_of(states[layer], gw[layer - 1])
        for h in range(2):
            v[h] = arrived(v[h], flying[h], slot - 1, h)
            scaled_rows = (v[h] * slopes[layer, span[h], :]).astype(bf16)
            flying[h], term = fine_half(slot, h, layer, scaled_rows)
            v[h] = v[h] + term
    local_copies[0].wait()
    for n in range(pieces):
        for d in peers:
            w_copies[0, n, d].wait_recv()
            block = cw.at[j, piece_of(from_peer[d - 1], n)]
            c_copies.append(remote(block, block, csend.at[d, n], crecv.at[d, n], partner))
            c_copies[-1].start()
    slopes[0] = slope_of(states[0], cw[j])
    for h in range(2):
        v[h] = arrived(v[h], flying[h], layers - 2, h)
        vbuf[span[h], :] = v[h]
        sbuf[span[h], :] = (v[h] * slopes[0, span[h], :]).astype(bf16)
    r0_copies = []
    s_far = sbuf[half_o, :]
    for c in range(2):
        far = step_size * back_product(s_far, cw[j, c * cols:(c + 1) * cols, :])
        r0s[c] = (far + jnp.where(j == c, vbuf[half_o, :], 0.0)).astype(bf16)
        r0_copies.append(remote(r0s.at[c], r0r.at[c], rsend.at[c], rrecv.at[c], partner))
        r0_copies[c].start()
    pending += r0_copies

    s_copies = []
    for d in peers:
        block = pl.ds(pl.multiple_of(to_peer[d - 1] * blk, blk), blk)
        s_copies.append(
            remote(states_in.at[:, :, block], stg.at[:, own_rows, :], ssend.at[d - 1],
                   srecv.at[d - 1], {"dp": to_peer[d - 1]})
        )
        s_copies[-1].start()

    own_states = pltpu.make_async_copy(
        states_in.at[:, :, own_in], stg.at[:, own_rows, :], osem.at[1]
    )
    own_states.start()

    s_near = sbuf[half_j, :]
    for c in range(2):
        near = step_size * back_product(s_near, cw[j, c * cols:(c + 1) * cols, :])
        near = near + jnp.where(j == c, vbuf[half_j, :], 0.0)
        resid[c] = near - guess[0, half_j, c * cols:(c + 1) * cols].astype(f32)
    chain = [
        remote(ebuf.at[c], inc.at[c], hsend.at[c], hrecv.at[c], {"layer": slab - 1})
        for c in range(2)
    ]

    pass_on = remote(inc.at[o], oinc, psend.at[0], precv.at[0], partner)

    @pl.when(jnp.logical_not(not_top))
    def _():
        inc[...] = jnp.zeros_like(inc)
        pass_on.start()

    for c in range(2):
        r0_copies[c].wait_recv()
        resid[c] = resid[c] + r0r[c].astype(f32)

        @pl.when(jnp.logical_not(not_top))
        def _():
            ebuf[c] = resid[c].astype(bf16)
            chain[c].start()

    for c_copy in c_copies:
        c_copy.wait_recv()
    cslopes[j] = slopes[0, half_j, :]
    cslopes[o] = slope_of(states[0, half_j, :], cw[o])

    @pl.when(not_top)
    def _():
        carried, products = [], [0.0, 0.0]
        for c in range(2):
            chain[c].wait_recv()
            if c == 1:
                pass_on.start()
            carried.append(inc[c].astype(f32))
            scaled_rows = (carried[c] * cslopes[c]).astype(bf16)
            for n in range(2):
                block = cw[c, n * cols:(n + 1) * cols, :]
                products[n] = products[n] + back_product(scaled_rows, block)
                if c == 1:
                    total = carried[n] + layers * step_size * products[n] + resid[n]
                    ebuf[n] = total.astype(bf16)

                    @pl.when(not_low)
                    def _():
                        chain[n].start()

    e_copy = remote(ebuf.at[o], oe, psend.at[1], precv.at[1], partner)
    e_copy.start()
    pending += [pass_on, e_copy]

    vbuf[half_j, :] = terminal[half_j, :] + inc[j].astype(f32)
    pass_on.wait_recv()
    vbuf[half_o, :] = terminal[half_o, :] + oinc[...].astype(f32)
    v = [vbuf[span[h], :] for h in range(2)]
    flying = [None, None]
    g_copies = {}

    own_scaled = []

    def spread(layer):
        for d in peers:
            g_copies[layer, d] = remote(
                sown.at[layer], sg.at[layer, own_rows],
                gsend.at[layer, d - 1], grecv.at[layer, d - 1], {"dp": to_peer[d - 1]},
            )
            g_copies[layer, d].start()
        own_scaled.append(
            pltpu.make_async_copy(sown.at[layer], sg.at[layer, own_rows], osem.at[2 + layer])
        )
        own_scaled[-1].start()

    for layer in range(layers - 1, -1, -1):
        slot = layers - 1 + (layers - 1 - layer)
        for h in range(2):
            v[h] = arrived(v[h], flying[h], slot - 1, h)
            scaled_rows = (v[h] * slopes[layer, span[h], :]).astype(bf16)
            sown[layer, span[h], :] = scaled_rows
            if layer < layers - 1:
                adjoint[layer + 1, span[h], :] = v[h].astype(bf16)
            if layer:
                flying[h], term = fine_half(slot, h, layer, scaled_rows)
                v[h] = v[h] + term
        spread(layer)
    e_copy.wait_recv()
    adjoint[0, half_j, :] = (guess[0, half_j, cols_j].astype(f32) + ebuf[j].astype(f32)).astype(bf16)
    adjoint[0, half_o, :] = (guess[0, half_o, cols_j].astype(f32) + oe[...].astype(f32)).astype(bf16)
    for copy in s_copies + list(g_copies.values()):
        copy.wait_recv()
    for copy in own_scaled + [own_states]:
        copy.wait()
    for copy in pending + c_copies + s_copies + list(w_copies.values()) + list(g_copies.values()):
        copy.wait_send()

    @pl.when(not_low)
    def _():
        point_copy.wait_send()
        for c in range(2):
            chain[c].wait_send()


def weight_gradients(inputs, scaled, adjoint_in, grads, adjoint):
    product = lax.dot_general(
        inputs[0], scaled[0], (((0,), (0,)), ((), ())), preferred_element_type=f32
    )
    grads[0] = step_size * product
    adjoint[...] = adjoint_in[...]


def solution(mesh):
    slab_count, dp_count, mp_count = (mesh.shape[a] for a in ("layer", "dp", "mp"))
    assert mp_count == 2

    def body(states, weights, guess_points, cotangent):
        layers, rows, width = states.shape
        blk, cols = weights.shape[1:]
        assert guess_points.shape[0] == 1
        half = rows // 2
        slots = 2 * (layers - 1)
        assert slab_count > 1 and layers > 1 and blk % 64 == 0
        all_rows = rows * dp_count
        dma = pltpu.SemaphoreType.DMA
        vmem = pl.BlockSpec(memory_space=pltpu.VMEM)
        anywhere = pl.BlockSpec(memory_space=pl.ANY)
        adjoint, scaled, inputs = pl.pallas_call(
            functools.partial(cycle, slab_count, dp_count, layers),
            out_shape=(
                jax.ShapeDtypeStruct((layers, rows, cols), bf16),
                jax.ShapeDtypeStruct((layers, all_rows, cols), bf16),
                jax.ShapeDtypeStruct((layers, all_rows, blk), bf16),
            ),
            in_specs=[anywhere, anywhere, vmem, vmem],
            out_specs=(vmem, anywhere, anywhere),
            scratch_shapes=[
                pltpu.VMEM((layers, rows, width), bf16),
                pltpu.VMEM((layers - 1, width, cols), bf16),
                pltpu.VMEM((2, width, cols), bf16),
                pltpu.VMEM((rows, cols), bf16),
                pltpu.VMEM((layers, rows, cols), f32),
                pltpu.VMEM((2, half, cols), f32),
                pltpu.VMEM((rows, cols), f32),
                pltpu.VMEM((rows, cols), bf16),
                pltpu.VMEM((rows, cols), f32),
                pltpu.VMEM((slots, 2, half, cols), bf16),
                pltpu.VMEM((slots, 2, half, cols), bf16),
                pltpu.VMEM((2, half, cols), bf16),
                pltpu.VMEM((2, half, cols), bf16),
                pltpu.VMEM((2, half, cols), f32),
                pltpu.VMEM((2, half, cols), bf16),
                pltpu.VMEM((half, cols), bf16),
                pltpu.VMEM((2, half, cols), bf16),
                pltpu.VMEM((half, cols), bf16),
                pltpu.VMEM((layers, rows, cols), bf16),
                dma((layers + 3, dp_count - 1)), dma((layers + 3, dp_count - 1)),
                dma((dp_count, 4)), dma((dp_count, 4)),
                dma((layers,)), dma((layers + 2,)),
                dma((dp_count - 1,)), dma((dp_count - 1,)),
                dma((layers, dp_count - 1)), dma((layers, dp_count - 1)),
                dma((slots, 2)), dma((slots, 2)),
                dma((2,)), dma((2,)),
                dma((2,)), dma((2,)),
                dma((1,)), dma((1,)),
                dma((2,)), dma((2,)),
            ],
            compiler_params=pltpu.CompilerParams(
                collective_id=0, has_side_effects=True, vmem_limit_bytes=56 * 2**20
            ),
            cost_estimate=pl.CostEstimate(
                flops=12 * layers * rows * width * cols, bytes_accessed=2**23, transcendentals=0
            ),
        )(states, weights, guess_points, cotangent)

        def per_layer(*shape):
            return pl.BlockSpec((1, *shape), lambda layer: (layer, 0, 0))

        grads, adjoint = pl.pallas_call(
            weight_gradients,
            grid=(layers,),
            out_shape=(
                jax.ShapeDtypeStruct((layers, blk, cols), f32),
                jax.ShapeDtypeStruct((layers, rows, cols), bf16),
            ),
            in_specs=[per_layer(all_rows, blk), per_layer(all_rows, cols), per_layer(rows, cols)],
            out_specs=(per_layer(blk, cols), per_layer(rows, cols)),
            compiler_params=pltpu.CompilerParams(vmem_limit_bytes=60 * 2**20),
        )(inputs, scaled, adjoint)
        return adjoint, grads

    return jax.shard_map(
        body,
        mesh=mesh,
        in_specs=(
            P("layer", "dp", None),
            P("layer", "dp", "mp"),
            P("layer", "dp", None),
            P("dp", None),
        ),
        out_specs=(P("layer", "dp", "mp"), P("layer", "dp", "mp")),
        check_vma=False,
    )
```

```python
import functools

import jax
import jax.numpy as jnp
from jax import lax
from jax.experimental import pallas as pl
from jax.experimental.pallas import tpu as pltpu
from jax.sharding import PartitionSpec as P

step_size = 0.1
f32, bf16 = jnp.float32, jnp.bfloat16
MESH = pl.DeviceIdType.MESH


def back_product(scaled_rows, turned_block):
    return jnp.dot(scaled_rows, turned_block, preferred_element_type=f32)


def slope_of(inputs, weight_block):
    tangent = jnp.tanh(jnp.dot(inputs, weight_block, preferred_element_type=f32))
    return 1.0 - tangent * tangent


def cycle(
    slab_count, dp_count, layers,
    states_in, weights, guess, cotangent, adjoint, sg, stg,
    states, gw, cw, wt, cwt, npt, slopes, cslopes, vbuf, sbuf, terminal,
    exs, exr, r0s, r0r, resid, inc, oinc, ebuf, oe, sown,
    wsend, wrecv, csend, crecv, lsem, osem, ssend, srecv, gsend, grecv,
    xsend, xrecv, rsend, rrecv, psend, precv, nsend, nrecv, hsend, hrecv,
):
    slab, mine, j = lax.axis_index("layer"), lax.axis_index("dp"), lax.axis_index("mp")
    o = 1 - j
    rows, width = states.shape[1], states.shape[2]
    blk, cols = weights.shape[1], weights.shape[2]
    half = rows // 2
    peers = range(1, dp_count)
    to_peer = [lax.rem(mine + d, dp_count) for d in peers]
    from_peer = [lax.rem(mine + dp_count - d, dp_count) for d in peers]
    not_top, not_low = slab < slab_count - 1, slab > 0
    own_in = pl.ds(pl.multiple_of(mine * blk, blk), blk)
    own_rows = pl.ds(pl.multiple_of(mine * rows, rows), rows)
    half_j = pl.ds(pl.multiple_of(j * half, half), half)
    half_o = pl.ds(pl.multiple_of(o * half, half), half)
    cols_j = pl.ds(pl.multiple_of(j * cols, cols), cols)
    cols_o = pl.ds(pl.multiple_of(o * cols, cols), cols)

    def remote(src, dst, send, recv, device):
        return pltpu.make_async_remote_copy(
            src_ref=src, dst_ref=dst, send_sem=send, recv_sem=recv,
            device_id=device, device_id_type=MESH,
        )

    barrier = pltpu.get_barrier_semaphore()

    def greet(device):
        pl.semaphore_signal(barrier, inc=1, device_id=device, device_id_type=MESH)

    for peer in to_peer:
        greet({"dp": peer})
    greet({"mp": o})

    @pl.when(not_top)
    def _():
        greet({"layer": slab + 1})

    @pl.when(not_low)
    def _():
        greet({"layer": slab - 1})

    pl.semaphore_wait(
        barrier, dp_count + not_top.astype(jnp.int32) + not_low.astype(jnp.int32)
    )

    states_copy = pltpu.make_async_copy(states_in, states, osem.at[0])
    states_copy.start()

    def home(layer):
        return cw.at[j] if layer == 0 else gw.at[layer - 1]

    partner = {"mp": o}
    point_copy = remote(guess.at[0, :, cols_j], npt, nsend.at[0], nrecv.at[0], {"layer": slab - 1})

    @pl.when(not_low)
    def _():
        point_copy.start()

    w_copies, local_copies = {}, {}
    pieces = 4
    piece = blk // pieces

    def piece_of(owner, n):
        return pl.ds(pl.multiple_of(owner * blk + n * piece, piece), piece)

    c_copies = [remote(weights.at[0], cw.at[j, own_in], csend.at[0, 0], crecv.at[0, 0], partner)]
    c_copies[0].start()
    order = range(layers - 1, -1, -1)
    for layer in order:
        parts = pieces if layer == 0 else 1
        for n in range(parts):
            for d in peers:
                source = weights.at[layer, n * piece:(n + 1) * piece] if layer == 0 else weights.at[layer]
                target = cw.at[j, piece_of(mine, n)] if layer == 0 else home(layer).at[own_in]
                sem = pieces - 1 + layer if layer else n
                w_copies[layer, n, d] = remote(
                    source, target, wsend.at[sem, d - 1], wrecv.at[sem, d - 1],
                    {"dp": to_peer[d - 1]},
                )
                w_copies[layer, n, d].start()
    for layer in order:
        local_copies[layer] = pltpu.make_async_copy(
            weights.at[layer], home(layer).at[own_in], lsem.at[layer]
        )
        local_copies[layer].start()

    @pl.when(not_top)
    def _():
        point_copy.wait_recv()
        terminal[...] = npt[...].astype(f32)

    @pl.when(jnp.logical_not(not_top))
    def _():
        terminal[...] = cotangent[:, cols_j].astype(f32)

    pending = []
    span = [slice(0, half), slice(half, 2 * half)]

    def fine_half(slot, h, layer, scaled_rows):
        w = wt.at[layer - 1]
        exs[slot, h] = (step_size * back_product(scaled_rows, w[:, cols_o])).astype(bf16)
        copy = remote(
            exs.at[slot, h], exr.at[slot, h], xsend.at[slot, h], xrecv.at[slot, h], partner
        )
        copy.start()
        pending.append(copy)
        return copy, step_size * back_product(scaled_rows, w[:, cols_j])

    def arrived(value, copy, slot, h):
        if copy is None:
            return value
        copy.wait_recv()
        return value + exr[slot, h].astype(f32)

    v = [terminal[span[h], :] for h in range(2)]
    flying = [None, None]
    states_copy.wait()
    for slot, layer in enumerate(range(layers - 1, 0, -1)):
        local_copies[layer].wait()
        for d in peers:
            w_copies[layer, 0, d].wait_recv()
        wt[layer - 1] = gw[layer - 1].T
        slopes[layer] = slope_of(states[layer], gw[layer - 1])
        for h in range(2):
            v[h] = arrived(v[h], flying[h], slot - 1, h)
            scaled_rows = (v[h] * slopes[layer, span[h], :]).astype(bf16)
            flying[h], term = fine_half(slot, h, layer, scaled_rows)
            v[h] = v[h] + term
    local_copies[0].wait()
    cwt[j, :, own_in] = cw[j, own_in, :].T
    for n in range(pieces):
        for d in peers:
            w_copies[0, n, d].wait_recv()
            block = cw.at[j, piece_of(from_peer[d - 1], n)]
            c_copies.append(remote(block, block, csend.at[d, n], crecv.at[d, n], partner))
            c_copies[-1].start()
            if piece % 128 == 0:
                landed = piece_of(from_peer[d - 1], n)
                cwt[j, :, landed] = cw[j, landed, :].T
    if piece % 128:
        cwt[j] = cw[j].T
    slopes[0] = slope_of(states[0], cw[j])
    for h in range(2):
        v[h] = arrived(v[h], flying[h], layers - 2, h)
        vbuf[span[h], :] = v[h]
        sbuf[span[h], :] = (v[h] * slopes[0, span[h], :]).astype(bf16)
    r0_copies = []
    s_far = sbuf[half_o, :]
    for c in range(2):
        far = step_size * back_product(s_far, cwt[j, :, c * cols:(c + 1) * cols])
        r0s[c] = (far + jnp.where(j == c, vbuf[half_o, :], 0.0)).astype(bf16)
        r0_copies.append(remote(r0s.at[c], r0r.at[c], rsend.at[c], rrecv.at[c], partner))
        r0_copies[c].start()
    pending += r0_copies

    s_copies = []
    for d in peers:
        block = pl.ds(pl.multiple_of(to_peer[d - 1] * blk, blk), blk)
        s_copies.append(
            remote(states_in.at[:, :, block], stg.at[:, own_rows, :], ssend.at[d - 1],
                   srecv.at[d - 1], {"dp": to_peer[d - 1]})
        )
        s_copies[-1].start()

    own_states = pltpu.make_async_copy(
        states_in.at[:, :, own_in], stg.at[:, own_rows, :], osem.at[1]
    )
    own_states.start()

    s_near = sbuf[half_j, :]
    for c in range(2):
        near = step_size * back_product(s_near, cwt[j, :, c * cols:(c + 1) * cols])
        near = near + jnp.where(j == c, vbuf[half_j, :], 0.0)
        resid[c] = near - guess[0, half_j, c * cols:(c + 1) * cols].astype(f32)
    chain = [
        remote(ebuf.at[c], inc.at[c], hsend.at[c], hrecv.at[c], {"layer": slab - 1})
        for c in range(2)
    ]

    pass_on = remote(inc.at[o], oinc, psend.at[0], precv.at[0], partner)

    @pl.when(jnp.logical_not(not_top))
    def _():
        inc[...] = jnp.zeros_like(inc)
        pass_on.start()

    for c in range(2):
        r0_copies[c].wait_recv()
        resid[c] = resid[c] + r0r[c].astype(f32)

        @pl.when(jnp.logical_not(not_top))
        def _():
            ebuf[c] = resid[c].astype(bf16)
            chain[c].start()

    for c_copy in c_copies:
        c_copy.wait_recv()
    cslopes[j] = slopes[0, half_j, :]
    cslopes[o] = slope_of(states[0, half_j, :], cw[o])
    cwt[o] = cw[o].T

    @pl.when(not_top)
    def _():
        carried, products = [], [0.0, 0.0]
        for c in range(2):
            chain[c].wait_recv()
            if c == 1:
                pass_on.start()
            carried.append(inc[c].astype(f32))
            scaled_rows = (carried[c] * cslopes[c]).astype(bf16)
            for n in range(2):
                block = cwt[c, :, n * cols:(n + 1) * cols]
                products[n] = products[n] + back_product(scaled_rows, block)
                if c == 1:
                    total = carried[n] + layers * step_size * products[n] + resid[n]
                    ebuf[n] = total.astype(bf16)

                    @pl.when(not_low)
                    def _():
                        chain[n].start()

    e_copy = remote(ebuf.at[o], oe, psend.at[1], precv.at[1], partner)
    e_copy.start()
    pending += [pass_on, e_copy]

    vbuf[half_j, :] = terminal[half_j, :] + inc[j].astype(f32)
    pass_on.wait_recv()
    vbuf[half_o, :] = terminal[half_o, :] + oinc[...].astype(f32)
    v = [vbuf[span[h], :] for h in range(2)]
    flying = [None, None]
    g_copies = {}

    own_scaled = []

    def spread(layer):
        for d in peers:
            g_copies[layer, d] = remote(
                sown.at[layer], sg.at[layer, own_rows],
                gsend.at[layer, d - 1], grecv.at[layer, d - 1], {"dp": to_peer[d - 1]},
            )
            g_copies[layer, d].start()
        own_scaled.append(
            pltpu.make_async_copy(sown.at[layer], sg.at[layer, own_rows], osem.at[2 + layer])
        )
        own_scaled[-1].start()

    for layer in range(layers - 1, -1, -1):
        slot = layers - 1 + (layers - 1 - layer)
        for h in range(2):
            v[h] = arrived(v[h], flying[h], slot - 1, h)
            scaled_rows = (v[h] * slopes[layer, span[h], :]).astype(bf16)
            sown[layer, span[h], :] = scaled_rows
            if layer < layers - 1:
                adjoint[layer + 1, span[h], :] = v[h].astype(bf16)
            if layer:
                flying[h], term = fine_half(slot, h, layer, scaled_rows)
                v[h] = v[h] + term
        spread(layer)
    e_copy.wait_recv()
    adjoint[0, half_j, :] = (guess[0, half_j, cols_j].astype(f32) + ebuf[j].astype(f32)).astype(bf16)
    adjoint[0, half_o, :] = (guess[0, half_o, cols_j].astype(f32) + oe[...].astype(f32)).astype(bf16)
    for copy in s_copies + list(g_copies.values()):
        copy.wait_recv()
    for copy in own_scaled + [own_states]:
        copy.wait()
    for copy in pending + c_copies + s_copies + list(w_copies.values()) + list(g_copies.values()):
        copy.wait_send()

    @pl.when(not_low)
    def _():
        point_copy.wait_send()
        for c in range(2):
            chain[c].wait_send()


def weight_gradients(inputs, scaled, adjoint_in, grads, adjoint):
    product = lax.dot_general(
        inputs[0], scaled[0], (((0,), (0,)), ((), ())), preferred_element_type=f32
    )
    grads[0] = step_size * product
    adjoint[...] = adjoint_in[...]


def solution(mesh):
    slab_count, dp_count, mp_count = (mesh.shape[a] for a in ("layer", "dp", "mp"))
    assert mp_count == 2

    def body(states, weights, guess_points, cotangent):
        layers, rows, width = states.shape
        blk, cols = weights.shape[1:]
        assert guess_points.shape[0] == 1
        half = rows // 2
        slots = 2 * (layers - 1)
        assert slab_count > 1 and layers > 1 and blk % 64 == 0
        all_rows = rows * dp_count
        dma = pltpu.SemaphoreType.DMA
        vmem = pl.BlockSpec(memory_space=pltpu.VMEM)
        anywhere = pl.BlockSpec(memory_space=pl.ANY)
        adjoint, scaled, inputs = pl.pallas_call(
            functools.partial(cycle, slab_count, dp_count, layers),
            out_shape=(
                jax.ShapeDtypeStruct((layers, rows, cols), bf16),
                jax.ShapeDtypeStruct((layers, all_rows, cols), bf16),
                jax.ShapeDtypeStruct((layers, all_rows, blk), bf16),
            ),
            in_specs=[anywhere, anywhere, vmem, vmem],
            out_specs=(vmem, anywhere, anywhere),
            scratch_shapes=[
                pltpu.VMEM((layers, rows, width), bf16),
                pltpu.VMEM((layers - 1, width, cols), bf16),
                pltpu.VMEM((2, width, cols), bf16),
                pltpu.VMEM((layers - 1, cols, width), bf16),
                pltpu.VMEM((2, cols, width), bf16),
                pltpu.VMEM((rows, cols), bf16),
                pltpu.VMEM((layers, rows, cols), f32),
                pltpu.VMEM((2, half, cols), f32),
                pltpu.VMEM((rows, cols), f32),
                pltpu.VMEM((rows, cols), bf16),
                pltpu.VMEM((rows, cols), f32),
                pltpu.VMEM((slots, 2, half, cols), bf16),
                pltpu.VMEM((slots, 2, half, cols), bf16),
                pltpu.VMEM((2, half, cols), bf16),
                pltpu.VMEM((2, half, cols), bf16),
                pltpu.VMEM((2, half, cols), f32),
                pltpu.VMEM((2, half, cols), bf16),
                pltpu.VMEM((half, cols), bf16),
                pltpu.VMEM((2, half, cols), bf16),
                pltpu.VMEM((half, cols), bf16),
                pltpu.VMEM((layers, rows, cols), bf16),
                dma((layers + 3, dp_count - 1)), dma((layers + 3, dp_count - 1)),
                dma((dp_count, 4)), dma((dp_count, 4)),
                dma((layers,)), dma((layers + 2,)),
                dma((dp_count - 1,)), dma((dp_count - 1,)),
                dma((layers, dp_count - 1)), dma((layers, dp_count - 1)),
                dma((slots, 2)), dma((slots, 2)),
                dma((2,)), dma((2,)),
                dma((2,)), dma((2,)),
                dma((1,)), dma((1,)),
                dma((2,)), dma((2,)),
            ],
            compiler_params=pltpu.CompilerParams(
                collective_id=0, has_side_effects=True, vmem_limit_bytes=56 * 2**20
            ),
            cost_estimate=pl.CostEstimate(
                flops=12 * layers * rows * width * cols, bytes_accessed=2**23, transcendentals=0
            ),
        )(states, weights, guess_points, cotangent)

        def per_layer(*shape):
            return pl.BlockSpec((1, *shape), lambda layer: (layer, 0, 0))

        grads, adjoint = pl.pallas_call(
            weight_gradients,
            grid=(layers,),
            out_shape=(
                jax.ShapeDtypeStruct((layers, blk, cols), f32),
                jax.ShapeDtypeStruct((layers, rows, cols), bf16),
            ),
            in_specs=[per_layer(all_rows, blk), per_layer(all_rows, cols), per_layer(rows, cols)],
            out_specs=(per_layer(blk, cols), per_layer(rows, cols)),
            compiler_params=pltpu.CompilerParams(vmem_limit_bytes=60 * 2**20),
        )(inputs, scaled, adjoint)
        return adjoint, grads

    return jax.shard_map(
        body,
        mesh=mesh,
        in_specs=(
            P("layer", "dp", None),
            P("layer", "dp", "mp"),
            P("layer", "dp", None),
            P("dp", None),
        ),
        out_specs=(P("layer", "dp", "mp"), P("layer", "dp", "mp")),
        check_vma=False,
    )
```

```python
import functools

import jax
import jax.numpy as jnp
from jax import lax
from jax.experimental import pallas as pl
from jax.experimental.pallas import tpu as pltpu
from jax.sharding import PartitionSpec as P

step_size = 0.1
f32, bf16 = jnp.float32, jnp.bfloat16
MESH = pl.DeviceIdType.MESH


def back_product(scaled_rows, turned_block):
    return jnp.dot(scaled_rows, turned_block, preferred_element_type=f32)


def back_product_raw(scaled_rows, weight_block):
    return lax.dot_general(
        scaled_rows, weight_block, (((1,), (1,)), ((), ())), preferred_element_type=f32
    )


def slope_of(inputs, weight_block):
    tangent = jnp.tanh(jnp.dot(inputs, weight_block, preferred_element_type=f32))
    return 1.0 - tangent * tangent


def cycle(
    slab_count, dp_count, layers,
    states_in, weights, guess, cotangent, adjoint, sg, stg,
    states, gw, cw, wt, npt, slopes, cslopes, vbuf, sbuf, terminal,
    exs, exr, r0s, r0r, resid, pair_slopes, pair_resid, errs, spread_errs, sown,
    wsend, wrecv, csend, crecv, lsem, osem, ssend, srecv, gsend, grecv,
    xsend, xrecv, rsend, rrecv, ksend, krecv, psend, precv, qsend, qrecv, nsend, nrecv, hsend, hrecv,
):
    slab, mine, j = lax.axis_index("layer"), lax.axis_index("dp"), lax.axis_index("mp")
    o = 1 - j
    rows, width = states.shape[1], states.shape[2]
    blk, cols = weights.shape[1], weights.shape[2]
    half = rows // 2
    peers = range(1, dp_count)
    to_peer = [lax.rem(mine + d, dp_count) for d in peers]
    from_peer = [lax.rem(mine + dp_count - d, dp_count) for d in peers]
    not_top, not_low = slab < slab_count - 1, slab > 0
    core = lax.rem(slab, 2)
    sibling = slab + 1 - 2 * core
    pair_not_top, pair_not_low = slab < slab_count - 2, slab > 1
    quarter = half // 2
    keep = pl.ds(pl.multiple_of(core * quarter, quarter), quarter)
    give = pl.ds(pl.multiple_of((1 - core) * quarter, quarter), quarter)
    own_in = pl.ds(pl.multiple_of(mine * blk, blk), blk)
    own_rows = pl.ds(pl.multiple_of(mine * rows, rows), rows)
    half_j = pl.ds(pl.multiple_of(j * half, half), half)
    half_o = pl.ds(pl.multiple_of(o * half, half), half)
    cols_j = pl.ds(pl.multiple_of(j * cols, cols), cols)
    cols_o = pl.ds(pl.multiple_of(o * cols, cols), cols)

    def remote(src, dst, send, recv, device):
        return pltpu.make_async_remote_copy(
            src_ref=src, dst_ref=dst, send_sem=send, recv_sem=recv,
            device_id=device, device_id_type=MESH,
        )

    barrier = pltpu.get_barrier_semaphore()

    def greet(device):
        pl.semaphore_signal(barrier, inc=1, device_id=device, device_id_type=MESH)

    for peer in to_peer:
        greet({"dp": peer})
    greet({"mp": o})
    greet({"layer": sibling})
    greet({"layer": sibling, "mp": o})

    @pl.when(pair_not_top)
    def _():
        greet({"layer": slab + 2})

    @pl.when(pair_not_low)
    def _():
        greet({"layer": slab - 2})

    @pl.when(not_top)
    def _():
        greet({"layer": slab + 1})

    @pl.when(not_low)
    def _():
        greet({"layer": slab - 1})

    greeted = dp_count + 2
    for there in (not_top, not_low, pair_not_top, pair_not_low):
        greeted = greeted + there.astype(jnp.int32)
    pl.semaphore_wait(barrier, greeted)

    states_copy = pltpu.make_async_copy(states_in, states, osem.at[0])
    states_copy.start()

    def home(layer):
        return cw.at[core, j] if layer == 0 else gw.at[layer - 1]

    partner, twin = {"mp": o}, {"layer": sibling}
    point_copy = remote(guess.at[0, :, cols_j], npt, nsend.at[0], nrecv.at[0], {"layer": slab - 1})

    @pl.when(not_low)
    def _():
        point_copy.start()

    w_copies, local_copies = {}, {}
    pieces = 4
    piece = blk // pieces

    def piece_of(owner, n):
        return pl.ds(pl.multiple_of(owner * blk + n * piece, piece), piece)

    c_copies = [remote(weights.at[0], cw.at[core, j, own_in], csend.at[0, 0], crecv.at[0, 0], partner)]
    c_copies[0].start()
    c_blocks = [own_in]
    twin_copies = [
        remote(weights.at[0], cw.at[core, j, own_in], ksend.at[0, 0, 0], krecv.at[0, 0, 0], twin)
    ]
    twin_copies[0].start()
    order = range(layers - 1, -1, -1)
    for layer in order:
        parts = pieces if layer == 0 else 1
        for n in range(parts):
            for d in peers:
                source = weights.at[layer, n * piece:(n + 1) * piece] if layer == 0 else weights.at[layer]
                target = cw.at[core, j, piece_of(mine, n)] if layer == 0 else home(layer).at[own_in]
                sem = pieces - 1 + layer if layer else n
                w_copies[layer, n, d] = remote(
                    source, target, wsend.at[sem, d - 1], wrecv.at[sem, d - 1],
                    {"dp": to_peer[d - 1]},
                )
                w_copies[layer, n, d].start()
    for layer in order:
        local_copies[layer] = pltpu.make_async_copy(
            weights.at[layer], home(layer).at[own_in], lsem.at[layer]
        )
        local_copies[layer].start()

    @pl.when(not_top)
    def _():
        point_copy.wait_recv()
        terminal[...] = npt[...].astype(f32)

    @pl.when(jnp.logical_not(not_top))
    def _():
        terminal[...] = cotangent[:, cols_j].astype(f32)

    pending = []
    span = [slice(0, half), slice(half, 2 * half)]

    def fine_half(slot, h, layer, scaled_rows):
        w = wt.at[layer - 1]
        exs[slot, h] = (step_size * back_product(scaled_rows, w[:, cols_o])).astype(bf16)
        copy = remote(
            exs.at[slot, h], exr.at[slot, h], xsend.at[slot, h], xrecv.at[slot, h], partner
        )
        copy.start()
        pending.append(copy)
        return copy, step_size * back_product(scaled_rows, w[:, cols_j])

    def arrived(value, copy, slot, h):
        if copy is None:
            return value
        copy.wait_recv()
        return value + exr[slot, h].astype(f32)

    v = [terminal[span[h], :] for h in range(2)]
    flying = [None, None]
    states_copy.wait()
    for slot, layer in enumerate(range(layers - 1, 0, -1)):
        local_copies[layer].wait()
        for d in peers:
            w_copies[layer, 0, d].wait_recv()
        wt[layer - 1] = gw[layer - 1].T
        slopes[layer] = slope_of(states[layer], gw[layer - 1])
        for h in range(2):
            v[h] = arrived(v[h], flying[h], slot - 1, h)
            scaled_rows = (v[h] * slopes[layer, span[h], :]).astype(bf16)
            flying[h], term = fine_half(slot, h, layer, scaled_rows)
            v[h] = v[h] + term
    local_copies[0].wait()
    for n in range(pieces):
        for d in peers:
            w_copies[0, n, d].wait_recv()
            c_blocks.append(piece_of(from_peer[d - 1], n))
            block = cw.at[core, j, c_blocks[-1]]
            c_copies.append(remote(block, block, csend.at[d, n], crecv.at[d, n], partner))
            c_copies[-1].start()
            twin_copies.append(remote(block, block, ksend.at[0, d, n], krecv.at[0, d, n], twin))
            twin_copies[-1].start()
    slopes[0] = slope_of(states[0], cw[core, j])
    for h in range(2):
        v[h] = arrived(v[h], flying[h], layers - 2, h)
        vbuf[span[h], :] = v[h]
        sbuf[span[h], :] = (v[h] * slopes[0, span[h], :]).astype(bf16)
    r0_copies = []
    s_far = sbuf[half_o, :]
    for c in range(2):
        far = step_size * back_product_raw(s_far, cw[core, j, c * cols:(c + 1) * cols, :])
        r0s[c] = (far + jnp.where(j == c, vbuf[half_o, :], 0.0)).astype(bf16)
        r0_copies.append(remote(r0s.at[c], r0r.at[c], rsend.at[c], rrecv.at[c], partner))
        r0_copies[c].start()
    pending += r0_copies

    s_copies = []
    for d in peers:
        block = pl.ds(pl.multiple_of(to_peer[d - 1] * blk, blk), blk)
        s_copies.append(
            remote(states_in.at[:, :, block], stg.at[:, own_rows, :], ssend.at[d - 1],
                   srecv.at[d - 1], {"dp": to_peer[d - 1]})
        )
        s_copies[-1].start()

    own_states = pltpu.make_async_copy(
        states_in.at[:, :, own_in], stg.at[:, own_rows, :], osem.at[1]
    )
    own_states.start()

    s_near = sbuf[half_j, :]
    for c in range(2):
        near = step_size * back_product_raw(s_near, cw[core, j, c * cols:(c + 1) * cols, :])
        near = near + jnp.where(j == c, vbuf[half_j, :], 0.0)
        resid[c] = near - guess[0, half_j, c * cols:(c + 1) * cols].astype(f32)
    for c in range(2):
        r0_copies[c].wait_recv()
        resid[c] = resid[c] + r0r[c].astype(f32)
    pair_resid[core] = resid[:, keep, :]
    twin_copies.append(
        remote(resid.at[:, give], pair_resid.at[core], psend.at[0], precv.at[0], twin)
    )
    twin_copies[-1].start()
    for n, (c_copy, block) in enumerate(zip(c_copies, c_blocks)):
        c_copy.wait_recv()
        d, m = (0, 0) if n == 0 else (1 + (n - 1) % (dp_count - 1), (n - 1) // (dp_count - 1))
        part = cw.at[core, o, block]
        twin_copies.append(remote(part, part, ksend.at[1, d, m], krecv.at[1, d, m], twin))
        twin_copies[-1].start()
    cslopes[j] = slopes[0, half_j, :]
    cslopes[o] = slope_of(states[0, half_j, :], cw[core, o])
    pair_slopes[core] = cslopes[:, keep, :]
    twin_copies.append(
        remote(cslopes.at[:, give], pair_slopes.at[core], psend.at[1], precv.at[1], twin)
    )
    twin_copies[-1].start()
    for copy in twin_copies:
        copy.wait_recv()

    chain = [
        remote(errs.at[2, n], errs.at[0, n], hsend.at[n], hrecv.at[n], {"layer": slab - 2})
        for n in range(2)
    ]

    def coarse_step(parity, start, incoming=None, outgoing=None):
        carried, products = [], [0.0, 0.0]
        for c in range(2):
            if incoming is not None:
                incoming[c].wait_recv()
            carried.append(errs[start, c].astype(f32))
            scaled_rows = (carried[c] * pair_slopes[parity, c]).astype(bf16)
            for n in range(2):
                block = cw[parity, c, n * cols:(n + 1) * cols, :]
                products[n] = products[n] + back_product_raw(scaled_rows, block)
                if c == 1:
                    total = carried[n] + layers * step_size * products[n] + pair_resid[parity, n]
                    errs[start + 1, n] = total.astype(bf16)
                    if outgoing is not None:

                        @pl.when(pair_not_low)
                        def _():
                            outgoing[n].start()

    @pl.when(jnp.logical_not(pair_not_top))
    def _():
        errs[0] = jnp.zeros(errs.shape[1:], bf16)
        for n in range(2):
            errs[1, n] = pair_resid[1, n].astype(bf16)

    @pl.when(pair_not_top)
    def _():
        coarse_step(1, 0, incoming=chain)

    place = 2 * j + core

    def scatter(kind):
        spread_errs[kind, place] = errs[1 - core + kind, j]
        copies = []
        for n, (index, c, device) in enumerate((
            (core + kind, j, twin),
            (1 - core + kind, o, partner),
            (core + kind, o, {"layer": sibling, "mp": o}),
        )):
            copies.append(
                remote(errs.at[index, c], spread_errs.at[kind, place], qsend.at[kind, n],
                       qrecv.at[kind, n], device)
            )
            copies[-1].start()
        return copies

    in_copies = scatter(0)
    coarse_step(0, 1, outgoing=chain)
    own_copies = scatter(1)
    pending += in_copies + own_copies

    for copy in in_copies:
        copy.wait_recv()
    v = [
        terminal[span[h], :]
        + jnp.concatenate([spread_errs[0, 2 * h + t].astype(f32) for t in range(2)], 0)
        for h in range(2)
    ]
    flying = [None, None]
    g_copies = {}

    own_scaled = []

    def spread(layer):
        for d in peers:
            g_copies[layer, d] = remote(
                sown.at[layer], sg.at[layer, own_rows],
                gsend.at[layer, d - 1], grecv.at[layer, d - 1], {"dp": to_peer[d - 1]},
            )
            g_copies[layer, d].start()
        own_scaled.append(
            pltpu.make_async_copy(sown.at[layer], sg.at[layer, own_rows], osem.at[2 + layer])
        )
        own_scaled[-1].start()

    for layer in range(layers - 1, -1, -1):
        slot = layers - 1 + (layers - 1 - layer)
        for h in range(2):
            v[h] = arrived(v[h], flying[h], slot - 1, h)
            scaled_rows = (v[h] * slopes[layer, span[h], :]).astype(bf16)
            sown[layer, span[h], :] = scaled_rows
            if layer < layers - 1:
                adjoint[layer + 1, span[h], :] = v[h].astype(bf16)
            if layer:
                flying[h], term = fine_half(slot, h, layer, scaled_rows)
                v[h] = v[h] + term
        spread(layer)
    for copy in own_copies:
        copy.wait_recv()
    for q in range(4):
        lines = slice(q * quarter, (q + 1) * quarter)
        own = guess[0, lines, cols_j].astype(f32) + spread_errs[1, q].astype(f32)
        adjoint[0, lines, :] = own.astype(bf16)
    for copy in s_copies + list(g_copies.values()):
        copy.wait_recv()
    for copy in own_scaled + [own_states]:
        copy.wait()
    for copy in pending + c_copies + twin_copies + s_copies + list(w_copies.values()) + list(g_copies.values()):
        copy.wait_send()

    @pl.when(not_low)
    def _():
        point_copy.wait_send()

    @pl.when(pair_not_low)
    def _():
        for n in range(2):
            chain[n].wait_send()


def weight_gradients(inputs, scaled, adjoint_in, grads, adjoint):
    product = lax.dot_general(
        inputs[0], scaled[0], (((0,), (0,)), ((), ())), preferred_element_type=f32
    )
    grads[0] = step_size * product
    adjoint[...] = adjoint_in[...]


def solution(mesh):
    slab_count, dp_count, mp_count = (mesh.shape[a] for a in ("layer", "dp", "mp"))
    assert mp_count == 2

    def body(states, weights, guess_points, cotangent):
        layers, rows, width = states.shape
        blk, cols = weights.shape[1:]
        assert guess_points.shape[0] == 1
        half = rows // 2
        slots = 2 * (layers - 1)
        assert slab_count % 2 == 0 and layers > 1 and blk % 64 == 0
        all_rows = rows * dp_count
        dma = pltpu.SemaphoreType.DMA
        vmem = pl.BlockSpec(memory_space=pltpu.VMEM)
        anywhere = pl.BlockSpec(memory_space=pl.ANY)
        adjoint, scaled, inputs = pl.pallas_call(
            functools.partial(cycle, slab_count, dp_count, layers),
            out_shape=(
                jax.ShapeDtypeStruct((layers, rows, cols), bf16),
                jax.ShapeDtypeStruct((layers, all_rows, cols), bf16),
                jax.ShapeDtypeStruct((layers, all_rows, blk), bf16),
            ),
            in_specs=[anywhere, anywhere, vmem, vmem],
            out_specs=(vmem, anywhere, anywhere),
            scratch_shapes=[
                pltpu.VMEM((layers, rows, width), bf16),
                pltpu.VMEM((layers - 1, width, cols), bf16),
                pltpu.VMEM((2, 2, width, cols), bf16),
                pltpu.VMEM((layers - 1, cols, width), bf16),
                pltpu.VMEM((rows, cols), bf16),
                pltpu.VMEM((layers, rows, cols), f32),
                pltpu.VMEM((2, half, cols), f32),
                pltpu.VMEM((rows, cols), f32),
                pltpu.VMEM((rows, cols), bf16),
                pltpu.VMEM((rows, cols), f32),
                pltpu.VMEM((slots, 2, half, cols), bf16),
                pltpu.VMEM((slots, 2, half, cols), bf16),
                pltpu.VMEM((2, half, cols), bf16),
                pltpu.VMEM((2, half, cols), bf16),
                pltpu.VMEM((2, half, cols), f32),
                pltpu.VMEM((2, 2, half // 2, cols), f32),
                pltpu.VMEM((2, 2, half // 2, cols), f32),
                pltpu.VMEM((3, 2, half // 2, cols), bf16),
                pltpu.VMEM((2, 4, half // 2, cols), bf16),
                pltpu.VMEM((layers, rows, cols), bf16),
                dma((layers + 3, dp_count - 1)), dma((layers + 3, dp_count - 1)),
                dma((dp_count, 4)), dma((dp_count, 4)),
                dma((layers,)), dma((layers + 2,)),
                dma((dp_count - 1,)), dma((dp_count - 1,)),
                dma((layers, dp_count - 1)), dma((layers, dp_count - 1)),
                dma((slots, 2)), dma((slots, 2)),
                dma((2,)), dma((2,)),
                dma((2, dp_count, 4)), dma((2, dp_count, 4)),
                dma((2,)), dma((2,)),
                dma((2, 3)), dma((2, 3)),
                dma((1,)), dma((1,)),
                dma((2,)), dma((2,)),
            ],
            compiler_params=pltpu.CompilerParams(
                collective_id=0, has_side_effects=True, vmem_limit_bytes=56 * 2**20
            ),
            cost_estimate=pl.CostEstimate(
                flops=12 * layers * rows * width * cols, bytes_accessed=2**23, transcendentals=0
            ),
        )(states, weights, guess_points, cotangent)

        def per_layer(*shape):
            return pl.BlockSpec((1, *shape), lambda layer: (layer, 0, 0))

        grads, adjoint = pl.pallas_call(
            weight_gradients,
            grid=(layers,),
            out_shape=(
                jax.ShapeDtypeStruct((layers, blk, cols), f32),
                jax.ShapeDtypeStruct((layers, rows, cols), bf16),
            ),
            in_specs=[per_layer(all_rows, blk), per_layer(all_rows, cols), per_layer(rows, cols)],
            out_specs=(per_layer(blk, cols), per_layer(rows, cols)),
            compiler_params=pltpu.CompilerParams(vmem_limit_bytes=60 * 2**20),
        )(inputs, scaled, adjoint)
        return adjoint, grads

    return jax.shard_map(
        body,
        mesh=mesh,
        in_specs=(
            P("layer", "dp", None),
            P("layer", "dp", "mp"),
            P("layer", "dp", None),
            P("dp", None),
        ),
        out_specs=(P("layer", "dp", "mp"), P("layer", "dp", "mp")),
        check_vma=False,
    )
```

```python
import functools

import jax
import jax.numpy as jnp
from jax import lax
from jax.experimental import pallas as pl
from jax.experimental.pallas import tpu as pltpu
from jax.sharding import PartitionSpec as P

step_size = 0.1
f32, bf16 = jnp.float32, jnp.bfloat16
MESH = pl.DeviceIdType.MESH


def back_product(scaled_rows, turned_block):
    return jnp.dot(scaled_rows, turned_block, preferred_element_type=f32)


def back_product_raw(scaled_rows, weight_block):
    return lax.dot_general(
        scaled_rows, weight_block, (((1,), (1,)), ((), ())), preferred_element_type=f32
    )


def slope_of(inputs, weight_block):
    tangent = jnp.tanh(jnp.dot(inputs, weight_block, preferred_element_type=f32))
    return 1.0 - tangent * tangent


def cycle(
    slab_count, dp_count, layers,
    states_in, weights, guess, cotangent, adjoint, sg, stg,
    states, gw, cw, wt, npt, slopes, cslopes, vbuf, sbuf, terminal,
    exs, exr, r0s, r0r, resid, pair_slopes, pair_resid, errs, spread_errs, sown,
    wsend, wrecv, csend, crecv, lsem, osem, ssend, srecv, gsend, grecv,
    xsend, xrecv, rsend, rrecv, ksend, krecv, psend, precv, qsend, qrecv, nsend, nrecv, hsend, hrecv,
):
    slab, mine, j = lax.axis_index("layer"), lax.axis_index("dp"), lax.axis_index("mp")
    o = 1 - j
    rows, width = states.shape[1], states.shape[2]
    blk, cols = weights.shape[1], weights.shape[2]
    half = rows // 2
    peers = range(1, dp_count)
    to_peer = [lax.rem(mine + d, dp_count) for d in peers]
    from_peer = [lax.rem(mine + dp_count - d, dp_count) for d in peers]
    not_top, not_low = slab < slab_count - 1, slab > 0
    core = lax.rem(slab, 2)
    sibling = slab + 1 - 2 * core
    pair_not_top, pair_not_low = slab < slab_count - 2, slab > 1
    quarter = half // 2
    keep = pl.ds(pl.multiple_of(core * quarter, quarter), quarter)
    give = pl.ds(pl.multiple_of((1 - core) * quarter, quarter), quarter)
    own_in = pl.ds(pl.multiple_of(mine * blk, blk), blk)
    own_rows = pl.ds(pl.multiple_of(mine * rows, rows), rows)
    half_j = pl.ds(pl.multiple_of(j * half, half), half)
    half_o = pl.ds(pl.multiple_of(o * half, half), half)
    cols_j = pl.ds(pl.multiple_of(j * cols, cols), cols)
    cols_o = pl.ds(pl.multiple_of(o * cols, cols), cols)

    def remote(src, dst, send, recv, device):
        return pltpu.make_async_remote_copy(
            src_ref=src, dst_ref=dst, send_sem=send, recv_sem=recv,
            device_id=device, device_id_type=MESH,
        )

    barrier = pltpu.get_barrier_semaphore()

    def greet(device):
        pl.semaphore_signal(barrier, inc=1, device_id=device, device_id_type=MESH)

    for peer in to_peer:
        greet({"dp": peer})
    greet({"mp": o})
    greet({"layer": sibling})
    greet({"layer": sibling, "mp": o})

    @pl.when(pair_not_top)
    def _():
        greet({"layer": slab + 2})

    @pl.when(pair_not_low)
    def _():
        greet({"layer": slab - 2})

    @pl.when(not_top)
    def _():
        greet({"layer": slab + 1})

    @pl.when(not_low)
    def _():
        greet({"layer": slab - 1})

    greeted = dp_count + 2
    for there in (not_top, not_low, pair_not_top, pair_not_low):
        greeted = greeted + there.astype(jnp.int32)
    pl.semaphore_wait(barrier, greeted)

    states_copy = pltpu.make_async_copy(states_in, states, osem.at[0])
    states_copy.start()

    def home(layer):
        return cw.at[core, j] if layer == 0 else gw.at[layer - 1]

    partner, twin = {"mp": o}, {"layer": sibling}
    point_copy = remote(guess.at[0, :, cols_j], npt, nsend.at[0], nrecv.at[0], {"layer": slab - 1})

    @pl.when(not_low)
    def _():
        point_copy.start()

    w_copies, local_copies = {}, {}
    pieces = 4
    piece = blk // pieces

    def piece_of(owner, n):
        return pl.ds(pl.multiple_of(owner * blk + n * piece, piece), piece)

    c_copies = [remote(weights.at[0], cw.at[core, j, own_in], csend.at[0, 0], crecv.at[0, 0], partner)]
    c_copies[0].start()
    c_blocks = [own_in]
    twin_copies = [
        remote(weights.at[0], cw.at[core, j, own_in], ksend.at[0, 0, 0], krecv.at[0, 0, 0], twin)
    ]
    twin_copies[0].start()
    order = range(layers - 1, -1, -1)
    stream = [(layer, n) for layer in order for n in range(pieces)]
    for layer, n in stream:
        for d in peers:
            w_copies[layer, n, d] = remote(
                weights.at[layer, n * piece:(n + 1) * piece],
                home(layer).at[piece_of(mine, n)],
                wsend.at[layer * pieces + n, d - 1], wrecv.at[layer * pieces + n, d - 1],
                {"dp": to_peer[d - 1]},
            )

    def start_piece(index):
        if index < len(stream):
            for d in peers:
                w_copies[(*stream[index], d)].start()

    def receive_piece(layer, n):
        for d in peers:
            w_copies[layer, n, d].wait_recv()
        start_piece(stream.index((layer, n)) + window)

    window = 5
    for index in range(window):
        start_piece(index)
    for layer in order:
        local_copies[layer] = pltpu.make_async_copy(
            weights.at[layer], home(layer).at[own_in], lsem.at[layer]
        )
        local_copies[layer].start()

    @pl.when(not_top)
    def _():
        point_copy.wait_recv()
        terminal[...] = npt[...].astype(f32)

    @pl.when(jnp.logical_not(not_top))
    def _():
        terminal[...] = cotangent[:, cols_j].astype(f32)

    pending = []
    span = [slice(0, half), slice(half, 2 * half)]

    def fine_half(slot, h, layer, scaled_rows):
        w = wt.at[layer - 1]
        exs[slot, h] = (step_size * back_product(scaled_rows, w[:, cols_o])).astype(bf16)
        copy = remote(
            exs.at[slot, h], exr.at[slot, h], xsend.at[slot, h], xrecv.at[slot, h], partner
        )
        copy.start()
        pending.append(copy)
        return copy, step_size * back_product(scaled_rows, w[:, cols_j])

    def arrived(value, copy, slot, h):
        if copy is None:
            return value
        copy.wait_recv()
        return value + exr[slot, h].astype(f32)

    v = [terminal[span[h], :] for h in range(2)]
    flying = [None, None]
    states_copy.wait()
    for slot, layer in enumerate(range(layers - 1, 0, -1)):
        local_copies[layer].wait()
        for n in range(pieces):
            receive_piece(layer, n)
        wt[layer - 1] = gw[layer - 1].T
        slopes[layer] = slope_of(states[layer], gw[layer - 1])
        for h in range(2):
            v[h] = arrived(v[h], flying[h], slot - 1, h)
            scaled_rows = (v[h] * slopes[layer, span[h], :]).astype(bf16)
            flying[h], term = fine_half(slot, h, layer, scaled_rows)
            v[h] = v[h] + term
    local_copies[0].wait()
    for n in range(pieces):
        receive_piece(0, n)
        for d in peers:
            c_blocks.append(piece_of(from_peer[d - 1], n))
            block = cw.at[core, j, c_blocks[-1]]
            c_copies.append(remote(block, block, csend.at[d, n], crecv.at[d, n], partner))
            c_copies[-1].start()
            twin_copies.append(remote(block, block, ksend.at[0, d, n], krecv.at[0, d, n], twin))
            twin_copies[-1].start()
    slopes[0] = slope_of(states[0], cw[core, j])
    for h in range(2):
        v[h] = arrived(v[h], flying[h], layers - 2, h)
        vbuf[span[h], :] = v[h]
        sbuf[span[h], :] = (v[h] * slopes[0, span[h], :]).astype(bf16)
    r0_copies = []
    s_far = sbuf[half_o, :]
    for c in range(2):
        far = step_size * back_product_raw(s_far, cw[core, j, c * cols:(c + 1) * cols, :])
        r0s[c] = (far + jnp.where(j == c, vbuf[half_o, :], 0.0)).astype(bf16)
        r0_copies.append(remote(r0s.at[c], r0r.at[c], rsend.at[c], rrecv.at[c], partner))
        r0_copies[c].start()
    pending += r0_copies

    s_copies = []
    for d in peers:
        block = pl.ds(pl.multiple_of(to_peer[d - 1] * blk, blk), blk)
        s_copies.append(
            remote(states_in.at[:, :, block], stg.at[:, own_rows, :], ssend.at[d - 1],
                   srecv.at[d - 1], {"dp": to_peer[d - 1]})
        )
        s_copies[-1].start()

    own_states = pltpu.make_async_copy(
        states_in.at[:, :, own_in], stg.at[:, own_rows, :], osem.at[1]
    )
    own_states.start()

    s_near = sbuf[half_j, :]
    for c in range(2):
        near = step_size * back_product_raw(s_near, cw[core, j, c * cols:(c + 1) * cols, :])
        near = near + jnp.where(j == c, vbuf[half_j, :], 0.0)
        resid[c] = near - guess[0, half_j, c * cols:(c + 1) * cols].astype(f32)
    for c in range(2):
        r0_copies[c].wait_recv()
        resid[c] = resid[c] + r0r[c].astype(f32)
    pair_resid[core] = resid[:, keep, :]
    twin_copies.append(
        remote(resid.at[:, give], pair_resid.at[core], psend.at[0], precv.at[0], twin)
    )
    twin_copies[-1].start()
    for n, (c_copy, block) in enumerate(zip(c_copies, c_blocks)):
        c_copy.wait_recv()
        d, m = (0, 0) if n == 0 else (1 + (n - 1) % (dp_count - 1), (n - 1) // (dp_count - 1))
        part = cw.at[core, o, block]
        twin_copies.append(remote(part, part, ksend.at[1, d, m], krecv.at[1, d, m], twin))
        twin_copies[-1].start()
    cslopes[j] = slopes[0, half_j, :]
    cslopes[o] = slope_of(states[0, half_j, :], cw[core, o])
    pair_slopes[core] = cslopes[:, keep, :]
    twin_copies.append(
        remote(cslopes.at[:, give], pair_slopes.at[core], psend.at[1], precv.at[1], twin)
    )
    twin_copies[-1].start()
    for copy in twin_copies:
        copy.wait_recv()

    chain = [
        remote(errs.at[2, n], errs.at[0, n], hsend.at[n], hrecv.at[n], {"layer": slab - 2})
        for n in range(2)
    ]

    def coarse_step(parity, start, incoming=None, outgoing=None):
        carried, products = [], [0.0, 0.0]
        for c in range(2):
            if incoming is not None:
                incoming[c].wait_recv()
            carried.append(errs[start, c].astype(f32))
            scaled_rows = (carried[c] * pair_slopes[parity, c]).astype(bf16)
            for n in range(2):
                block = cw[parity, c, n * cols:(n + 1) * cols, :]
                products[n] = products[n] + back_product_raw(scaled_rows, block)
                if c == 1:
                    total = carried[n] + layers * step_size * products[n] + pair_resid[parity, n]
                    errs[start + 1, n] = total.astype(bf16)
                    if outgoing is not None:

                        @pl.when(pair_not_low)
                        def _():
                            outgoing[n].start()

    @pl.when(jnp.logical_not(pair_not_top))
    def _():
        errs[0] = jnp.zeros(errs.shape[1:], bf16)
        for n in range(2):
            errs[1, n] = pair_resid[1, n].astype(bf16)

    @pl.when(pair_not_top)
    def _():
        coarse_step(1, 0, incoming=chain)

    place = 2 * j + core

    def scatter(kind):
        spread_errs[kind, place] = errs[1 - core + kind, j]
        copies = []
        for n, (index, c, device) in enumerate((
            (core + kind, j, twin),
            (1 - core + kind, o, partner),
            (core + kind, o, {"layer": sibling, "mp": o}),
        )):
            copies.append(
                remote(errs.at[index, c], spread_errs.at[kind, place], qsend.at[kind, n],
                       qrecv.at[kind, n], device)
            )
            copies[-1].start()
        return copies

    in_copies = scatter(0)
    coarse_step(0, 1, outgoing=chain)
    own_copies = scatter(1)
    pending += in_copies + own_copies

    for copy in in_copies:
        copy.wait_recv()
    v = [
        terminal[span[h], :]
        + jnp.concatenate([spread_errs[0, 2 * h + t].astype(f32) for t in range(2)], 0)
        for h in range(2)
    ]
    flying = [None, None]
    g_copies = {}

    own_scaled = []

    def spread(layer):
        for d in peers:
            g_copies[layer, d] = remote(
                sown.at[layer], sg.at[layer, own_rows],
                gsend.at[layer, d - 1], grecv.at[layer, d - 1], {"dp": to_peer[d - 1]},
            )
            g_copies[layer, d].start()
        own_scaled.append(
            pltpu.make_async_copy(sown.at[layer], sg.at[layer, own_rows], osem.at[2 + layer])
        )
        own_scaled[-1].start()

    for layer in range(layers - 1, -1, -1):
        slot = layers - 1 + (layers - 1 - layer)
        for h in range(2):
            v[h] = arrived(v[h], flying[h], slot - 1, h)
            scaled_rows = (v[h] * slopes[layer, span[h], :]).astype(bf16)
            sown[layer, span[h], :] = scaled_rows
            if layer < layers - 1:
                adjoint[layer + 1, span[h], :] = v[h].astype(bf16)
            if layer:
                flying[h], term = fine_half(slot, h, layer, scaled_rows)
                v[h] = v[h] + term
        spread(layer)
    for copy in own_copies:
        copy.wait_recv()
    for q in range(4):
        lines = slice(q * quarter, (q + 1) * quarter)
        own = guess[0, lines, cols_j].astype(f32) + spread_errs[1, q].astype(f32)
        adjoint[0, lines, :] = own.astype(bf16)
    for copy in s_copies + list(g_copies.values()):
        copy.wait_recv()
    for copy in own_scaled + [own_states]:
        copy.wait()
    for copy in pending + c_copies + twin_copies + s_copies + list(w_copies.values()) + list(g_copies.values()):
        copy.wait_send()

    @pl.when(not_low)
    def _():
        point_copy.wait_send()

    @pl.when(pair_not_low)
    def _():
        for n in range(2):
            chain[n].wait_send()


def weight_gradients(inputs, scaled, adjoint_in, grads, adjoint):
    product = lax.dot_general(
        inputs[0], scaled[0], (((0,), (0,)), ((), ())), preferred_element_type=f32
    )
    grads[0] = step_size * product
    adjoint[...] = adjoint_in[...]


def solution(mesh):
    slab_count, dp_count, mp_count = (mesh.shape[a] for a in ("layer", "dp", "mp"))
    assert mp_count == 2

    def body(states, weights, guess_points, cotangent):
        layers, rows, width = states.shape
        blk, cols = weights.shape[1:]
        assert guess_points.shape[0] == 1
        half = rows // 2
        slots = 2 * (layers - 1)
        assert slab_count % 2 == 0 and layers > 1 and blk % 64 == 0
        all_rows = rows * dp_count
        dma = pltpu.SemaphoreType.DMA
        vmem = pl.BlockSpec(memory_space=pltpu.VMEM)
        anywhere = pl.BlockSpec(memory_space=pl.ANY)
        adjoint, scaled, inputs = pl.pallas_call(
            functools.partial(cycle, slab_count, dp_count, layers),
            out_shape=(
                jax.ShapeDtypeStruct((layers, rows, cols), bf16),
                jax.ShapeDtypeStruct((layers, all_rows, cols), bf16),
                jax.ShapeDtypeStruct((layers, all_rows, blk), bf16),
            ),
            in_specs=[anywhere, anywhere, vmem, vmem],
            out_specs=(vmem, anywhere, anywhere),
            scratch_shapes=[
                pltpu.VMEM((layers, rows, width), bf16),
                pltpu.VMEM((layers - 1, width, cols), bf16),
                pltpu.VMEM((2, 2, width, cols), bf16),
                pltpu.VMEM((layers - 1, cols, width), bf16),
                pltpu.VMEM((rows, cols), bf16),
                pltpu.VMEM((layers, rows, cols), f32),
                pltpu.VMEM((2, half, cols), f32),
                pltpu.VMEM((rows, cols), f32),
                pltpu.VMEM((rows, cols), bf16),
                pltpu.VMEM((rows, cols), f32),
                pltpu.VMEM((slots, 2, half, cols), bf16),
                pltpu.VMEM((slots, 2, half, cols), bf16),
                pltpu.VMEM((2, half, cols), bf16),
                pltpu.VMEM((2, half, cols), bf16),
                pltpu.VMEM((2, half, cols), f32),
                pltpu.VMEM((2, 2, half // 2, cols), f32),
                pltpu.VMEM((2, 2, half // 2, cols), f32),
                pltpu.VMEM((3, 2, half // 2, cols), bf16),
                pltpu.VMEM((2, 4, half // 2, cols), bf16),
                pltpu.VMEM((layers, rows, cols), bf16),
                dma((layers * 4, dp_count - 1)), dma((layers * 4, dp_count - 1)),
                dma((dp_count, 4)), dma((dp_count, 4)),
                dma((layers,)), dma((layers + 2,)),
                dma((dp_count - 1,)), dma((dp_count - 1,)),
                dma((layers, dp_count - 1)), dma((layers, dp_count - 1)),
                dma((slots, 2)), dma((slots, 2)),
                dma((2,)), dma((2,)),
                dma((2, dp_count, 4)), dma((2, dp_count, 4)),
                dma((2,)), dma((2,)),
                dma((2, 3)), dma((2, 3)),
                dma((1,)), dma((1,)),
                dma((2,)), dma((2,)),
            ],
            compiler_params=pltpu.CompilerParams(
                collective_id=0, has_side_effects=True, vmem_limit_bytes=56 * 2**20
            ),
            cost_estimate=pl.CostEstimate(
                flops=12 * layers * rows * width * cols, bytes_accessed=2**23, transcendentals=0
            ),
        )(states, weights, guess_points, cotangent)

        def per_layer(*shape):
            return pl.BlockSpec((1, *shape), lambda layer: (layer, 0, 0))

        grads, adjoint = pl.pallas_call(
            weight_gradients,
            grid=(layers,),
            out_shape=(
                jax.ShapeDtypeStruct((layers, blk, cols), f32),
                jax.ShapeDtypeStruct((layers, rows, cols), bf16),
            ),
            in_specs=[per_layer(all_rows, blk), per_layer(all_rows, cols), per_layer(rows, cols)],
            out_specs=(per_layer(blk, cols), per_layer(rows, cols)),
            compiler_params=pltpu.CompilerParams(vmem_limit_bytes=60 * 2**20),
        )(inputs, scaled, adjoint)
        return adjoint, grads

    return jax.shard_map(
        body,
        mesh=mesh,
        in_specs=(
            P("layer", "dp", None),
            P("layer", "dp", "mp"),
            P("layer", "dp", None),
            P("dp", None),
        ),
        out_specs=(P("layer", "dp", "mp"), P("layer", "dp", "mp")),
        check_vma=False,
    )
```

```python
import functools

import jax
import jax.numpy as jnp
from jax import lax
from jax.experimental import pallas as pl
from jax.experimental.pallas import tpu as pltpu
from jax.sharding import PartitionSpec as P

step_size = 0.1
f32, bf16 = jnp.float32, jnp.bfloat16
MESH = pl.DeviceIdType.MESH


def back_product(scaled_rows, turned_block):
    return jnp.dot(scaled_rows, turned_block, preferred_element_type=f32)


def back_product_raw(scaled_rows, weight_block):
    return lax.dot_general(
        scaled_rows, weight_block, (((1,), (1,)), ((), ())), preferred_element_type=f32
    )


def slope_of(inputs, weight_block):
    tangent = jnp.tanh(jnp.dot(inputs, weight_block, preferred_element_type=f32))
    return 1.0 - tangent * tangent


def cycle(
    slab_count, dp_count, layers,
    states_in, weights, guess, cotangent, adjoint, sg, stg,
    states, gw, cw, wt, npt, slopes, cslopes, vbuf, sbuf, terminal,
    exs, exr, r0s, r0r, resid, pair_slopes, pair_resid, errs, spread_errs, sown,
    wsend, wrecv, csend, crecv, lsem, osem, ssend, srecv, gsend, grecv,
    xsend, xrecv, rsend, rrecv, ksend, krecv, psend, precv, qsend, qrecv, nsend, nrecv, hsend, hrecv,
):
    slab, mine, j = lax.axis_index("layer"), lax.axis_index("dp"), lax.axis_index("mp")
    o = 1 - j
    rows, width = states.shape[1], states.shape[2]
    blk, cols = weights.shape[1], weights.shape[2]
    half = rows // 2
    peers = range(1, dp_count)
    to_peer = [lax.rem(mine + d, dp_count) for d in peers]
    from_peer = [lax.rem(mine + dp_count - d, dp_count) for d in peers]
    not_top, not_low = slab < slab_count - 1, slab > 0
    core = lax.rem(slab, 2)
    sibling = slab + 1 - 2 * core
    pair_not_top, pair_not_low = slab < slab_count - 2, slab > 1
    quarter = half // 2
    keep = pl.ds(pl.multiple_of(core * quarter, quarter), quarter)
    give = pl.ds(pl.multiple_of((1 - core) * quarter, quarter), quarter)
    own_in = pl.ds(pl.multiple_of(mine * blk, blk), blk)
    own_rows = pl.ds(pl.multiple_of(mine * rows, rows), rows)
    half_j = pl.ds(pl.multiple_of(j * half, half), half)
    half_o = pl.ds(pl.multiple_of(o * half, half), half)
    cols_j = pl.ds(pl.multiple_of(j * cols, cols), cols)
    cols_o = pl.ds(pl.multiple_of(o * cols, cols), cols)

    def remote(src, dst, send, recv, device):
        return pltpu.make_async_remote_copy(
            src_ref=src, dst_ref=dst, send_sem=send, recv_sem=recv,
            device_id=device, device_id_type=MESH,
        )

    barrier = pltpu.get_barrier_semaphore()

    def greet(device):
        pl.semaphore_signal(barrier, inc=1, device_id=device, device_id_type=MESH)

    for peer in to_peer:
        greet({"dp": peer})
    greet({"mp": o})
    greet({"layer": sibling})
    greet({"layer": sibling, "mp": o})

    @pl.when(pair_not_top)
    def _():
        greet({"layer": slab + 2})

    @pl.when(pair_not_low)
    def _():
        greet({"layer": slab - 2})

    @pl.when(not_top)
    def _():
        greet({"layer": slab + 1})

    @pl.when(not_low)
    def _():
        greet({"layer": slab - 1})

    greeted = dp_count + 2
    for there in (not_top, not_low, pair_not_top, pair_not_low):
        greeted = greeted + there.astype(jnp.int32)
    pl.semaphore_wait(barrier, greeted)

    states_copy = pltpu.make_async_copy(states_in, states, osem.at[0])
    states_copy.start()

    def home(layer):
        return cw.at[core, j] if layer == 0 else gw.at[layer - 1]

    partner, twin = {"mp": o}, {"layer": sibling}
    point_copy = remote(guess.at[0, :, cols_j], npt, nsend.at[0], nrecv.at[0], {"layer": slab - 1})

    @pl.when(not_low)
    def _():
        point_copy.start()

    w_copies, local_copies = {}, {}
    pieces = 4
    piece = blk // pieces

    def piece_of(owner, n):
        return pl.ds(pl.multiple_of(owner * blk + n * piece, piece), piece)

    c_copies = [remote(weights.at[0], cw.at[core, j, own_in], csend.at[0, 0], crecv.at[0, 0], partner)]
    c_copies[0].start()
    c_blocks = [own_in]
    twin_copies = [
        remote(weights.at[0], cw.at[core, j, own_in], ksend.at[0, 0, 0], krecv.at[0, 0, 0], twin)
    ]
    twin_copies[0].start()
    order = range(layers - 1, -1, -1)
    stream = [(layer, n) for layer in order for n in range(pieces)]
    for layer, n in stream:
        for d in peers:
            w_copies[layer, n, d] = remote(
                weights.at[layer, n * piece:(n + 1) * piece],
                home(layer).at[piece_of(mine, n)],
                wsend.at[layer * pieces + n, d - 1], wrecv.at[layer * pieces + n, d - 1],
                {"dp": to_peer[d - 1]},
            )

    def start_piece(index):
        if index < len(stream):
            for d in peers:
                w_copies[(*stream[index], d)].start()

    def receive_piece(layer, n):
        for d in peers:
            w_copies[layer, n, d].wait_recv()
        start_piece(stream.index((layer, n)) + window)

    window = 5
    for index in range(window):
        start_piece(index)
    for layer in order:
        local_copies[layer] = pltpu.make_async_copy(
            weights.at[layer], home(layer).at[own_in], lsem.at[layer]
        )
        local_copies[layer].start()

    @pl.when(not_top)
    def _():
        point_copy.wait_recv()
        terminal[...] = npt[...].astype(f32)

    @pl.when(jnp.logical_not(not_top))
    def _():
        terminal[...] = cotangent[:, cols_j].astype(f32)

    pending = []
    span = [slice(0, half), slice(half, 2 * half)]

    def fine_half(slot, h, layer, scaled_rows):
        w = wt.at[layer - 1]
        exs[slot, h] = (step_size * back_product(scaled_rows, w[:, cols_o])).astype(bf16)
        copy = remote(
            exs.at[slot, h], exr.at[slot, h], xsend.at[slot, h], xrecv.at[slot, h], partner
        )
        copy.start()
        pending.append(copy)
        return copy, step_size * back_product(scaled_rows, w[:, cols_j])

    def arrived(value, copy, slot, h):
        if copy is None:
            return value
        copy.wait_recv()
        return value + exr[slot, h].astype(f32)

    v = [terminal[span[h], :] for h in range(2)]
    flying = [None, None]
    states_copy.wait()
    for slot, layer in enumerate(range(layers - 1, 0, -1)):
        local_copies[layer].wait()
        for n in range(pieces):
            receive_piece(layer, n)
        wt[layer - 1] = gw[layer - 1].T
        slopes[layer] = slope_of(states[layer], gw[layer - 1])
        for h in range(2):
            v[h] = arrived(v[h], flying[h], slot - 1, h)
            scaled_rows = (v[h] * slopes[layer, span[h], :]).astype(bf16)
            flying[h], term = fine_half(slot, h, layer, scaled_rows)
            v[h] = v[h] + term
    local_copies[0].wait()
    for n in range(pieces):
        receive_piece(0, n)
        for d in peers:
            c_blocks.append(piece_of(from_peer[d - 1], n))
            block = cw.at[core, j, c_blocks[-1]]
            c_copies.append(remote(block, block, csend.at[d, n], crecv.at[d, n], partner))
            c_copies[-1].start()
            twin_copies.append(remote(block, block, ksend.at[0, d, n], krecv.at[0, d, n], twin))
            twin_copies[-1].start()
    slopes[0] = slope_of(states[0], cw[core, j])
    for h in range(2):
        v[h] = arrived(v[h], flying[h], layers - 2, h)
        vbuf[span[h], :] = v[h]
        sbuf[span[h], :] = (v[h] * slopes[0, span[h], :]).astype(bf16)
    r0_copies = []
    s_far = sbuf[half_o, :]
    for c in range(2):
        far = step_size * back_product_raw(s_far, cw[core, j, c * cols:(c + 1) * cols, :])
        r0s[c] = (far + jnp.where(j == c, vbuf[half_o, :], 0.0)).astype(bf16)
        r0_copies.append(remote(r0s.at[c], r0r.at[c], rsend.at[c], rrecv.at[c], partner))
        r0_copies[c].start()
    pending += r0_copies

    s_copies = []
    for d in peers:
        block = pl.ds(pl.multiple_of(to_peer[d - 1] * blk, blk), blk)
        s_copies.append(
            remote(states_in.at[:, :, block], stg.at[:, own_rows, :], ssend.at[d - 1],
                   srecv.at[d - 1], {"dp": to_peer[d - 1]})
        )
        s_copies[-1].start()

    own_states = pltpu.make_async_copy(
        states_in.at[:, :, own_in], stg.at[:, own_rows, :], osem.at[1]
    )
    own_states.start()

    s_near = sbuf[half_j, :]
    for c in range(2):
        near = step_size * back_product_raw(s_near, cw[core, j, c * cols:(c + 1) * cols, :])
        near = near + jnp.where(j == c, vbuf[half_j, :], 0.0)
        resid[c] = near - guess[0, half_j, c * cols:(c + 1) * cols].astype(f32)
    for c in range(2):
        r0_copies[c].wait_recv()
        resid[c] = resid[c] + r0r[c].astype(f32)
    pair_resid[core] = resid[:, keep, :]
    twin_copies.append(
        remote(resid.at[:, give], pair_resid.at[core], psend.at[0], precv.at[0], twin)
    )
    twin_copies[-1].start()
    for n, (c_copy, block) in enumerate(zip(c_copies, c_blocks)):
        c_copy.wait_recv()
        d, m = (0, 0) if n == 0 else (1 + (n - 1) % (dp_count - 1), (n - 1) // (dp_count - 1))
        part = cw.at[core, o, block]
        twin_copies.append(remote(part, part, ksend.at[1, d, m], krecv.at[1, d, m], twin))
        twin_copies[-1].start()
    cslopes[j] = slopes[0, half_j, :]
    cslopes[o] = slope_of(states[0, half_j, :], cw[core, o])
    pair_slopes[core] = cslopes[:, keep, :]
    twin_copies.append(
        remote(cslopes.at[:, give], pair_slopes.at[core], psend.at[1], precv.at[1], twin)
    )
    twin_copies[-1].start()
    for copy in twin_copies:
        copy.wait_recv()

    chain = [
        remote(errs.at[2, n], errs.at[0, n], hsend.at[n], hrecv.at[n], {"layer": slab - 2})
        for n in range(2)
    ]

    def coarse_step(parity, start, incoming=None, outgoing=None):
        carried, products = [], [0.0, 0.0]
        for c in range(2):
            if incoming is not None:
                incoming[c].wait_recv()
            carried.append(errs[start, c].astype(f32))
            scaled_rows = (carried[c] * pair_slopes[parity, c]).astype(bf16)
            for n in range(2):
                block = cw[parity, c, n * cols:(n + 1) * cols, :]
                products[n] = products[n] + back_product_raw(scaled_rows, block)
                if c == 1:
                    total = carried[n] + layers * step_size * products[n] + pair_resid[parity, n]
                    errs[start + 1, n] = total.astype(bf16)
                    if outgoing is not None:

                        @pl.when(pair_not_low)
                        def _():
                            outgoing[n].start()

    @pl.when(jnp.logical_not(pair_not_top))
    def _():
        errs[0] = jnp.zeros(errs.shape[1:], bf16)
        for n in range(2):
            errs[1, n] = pair_resid[1, n].astype(bf16)

    @pl.when(pair_not_top)
    def _():
        coarse_step(1, 0, incoming=chain)

    place = 2 * j + core

    def scatter(kind):
        spread_errs[kind, place] = errs[1 - core + kind, j]
        copies = []
        for n, (index, c, device) in enumerate((
            (core + kind, j, twin),
            (1 - core + kind, o, partner),
            (core + kind, o, {"layer": sibling, "mp": o}),
        )):
            copies.append(
                remote(errs.at[index, c], spread_errs.at[kind, place], qsend.at[kind, n],
                       qrecv.at[kind, n], device)
            )
            copies[-1].start()
        return copies

    @pl.when(pair_not_low)
    def _():
        coarse_step(0, 1, outgoing=chain)

    in_copies = scatter(0)
    early = pending + c_copies + twin_copies + list(w_copies.values())
    pending = list(in_copies)

    for copy in in_copies:
        copy.wait_recv()
    v = [
        terminal[span[h], :]
        + jnp.concatenate([spread_errs[0, 2 * h + t].astype(f32) for t in range(2)], 0)
        for h in range(2)
    ]
    flying = [None, None]
    g_copies = {}

    own_scaled = []

    def spread(layer):
        for d in peers:
            g_copies[layer, d] = remote(
                sown.at[layer], sg.at[layer, own_rows],
                gsend.at[layer, d - 1], grecv.at[layer, d - 1], {"dp": to_peer[d - 1]},
            )
            g_copies[layer, d].start()
        own_scaled.append(
            pltpu.make_async_copy(sown.at[layer], sg.at[layer, own_rows], osem.at[2 + layer])
        )
        own_scaled[-1].start()

    for layer in range(layers - 1, -1, -1):
        slot = layers - 1 + (layers - 1 - layer)
        for h in range(2):
            v[h] = arrived(v[h], flying[h], slot - 1, h)
            scaled_rows = (v[h] * slopes[layer, span[h], :]).astype(bf16)
            sown[layer, span[h], :] = scaled_rows
            if layer < layers - 1:
                adjoint[layer + 1, span[h], :] = v[h].astype(bf16)
            if layer:
                flying[h], term = fine_half(slot, h, layer, scaled_rows)
                v[h] = v[h] + term
        spread(layer)
        if layer == layers - 1:
            for copy in early[:len(early) // 2]:
                copy.wait_send()
        if layer == max(layers - 2, 1):
            for copy in early[len(early) // 2:]:
                copy.wait_send()
        if layer == 1:

            @pl.when(jnp.logical_not(pair_not_low))
            def _():
                coarse_step(0, 1)

            own_copies = scatter(1)
            pending += own_copies
    for copy in own_copies:
        copy.wait_recv()
    for q in range(4):
        lines = slice(q * quarter, (q + 1) * quarter)
        own = guess[0, lines, cols_j].astype(f32) + spread_errs[1, q].astype(f32)
        adjoint[0, lines, :] = own.astype(bf16)
    for copy in s_copies + list(g_copies.values()):
        copy.wait_recv()
    for copy in own_scaled + [own_states]:
        copy.wait()
    for copy in pending + s_copies + list(g_copies.values()):
        copy.wait_send()

    @pl.when(not_low)
    def _():
        point_copy.wait_send()

    @pl.when(pair_not_low)
    def _():
        for n in range(2):
            chain[n].wait_send()


def weight_gradients(inputs, scaled, adjoint_in, grads, adjoint):
    product = lax.dot_general(
        inputs[0], scaled[0], (((0,), (0,)), ((), ())), preferred_element_type=f32
    )
    grads[0] = step_size * product
    adjoint[...] = adjoint_in[...]


def solution(mesh):
    slab_count, dp_count, mp_count = (mesh.shape[a] for a in ("layer", "dp", "mp"))
    assert mp_count == 2

    def body(states, weights, guess_points, cotangent):
        layers, rows, width = states.shape
        blk, cols = weights.shape[1:]
        assert guess_points.shape[0] == 1
        half = rows // 2
        slots = 2 * (layers - 1)
        assert slab_count % 2 == 0 and layers > 1 and blk % 64 == 0
        all_rows = rows * dp_count
        dma = pltpu.SemaphoreType.DMA
        vmem = pl.BlockSpec(memory_space=pltpu.VMEM)
        anywhere = pl.BlockSpec(memory_space=pl.ANY)
        adjoint, scaled, inputs = pl.pallas_call(
            functools.partial(cycle, slab_count, dp_count, layers),
            out_shape=(
                jax.ShapeDtypeStruct((layers, rows, cols), bf16),
                jax.ShapeDtypeStruct((layers, all_rows, cols), bf16),
                jax.ShapeDtypeStruct((layers, all_rows, blk), bf16),
            ),
            in_specs=[anywhere, anywhere, vmem, vmem],
            out_specs=(vmem, anywhere, anywhere),
            scratch_shapes=[
                pltpu.VMEM((layers, rows, width), bf16),
                pltpu.VMEM((layers - 1, width, cols), bf16),
                pltpu.VMEM((2, 2, width, cols), bf16),
                pltpu.VMEM((layers - 1, cols, width), bf16),
                pltpu.VMEM((rows, cols), bf16),
                pltpu.VMEM((layers, rows, cols), f32),
                pltpu.VMEM((2, half, cols), f32),
                pltpu.VMEM((rows, cols), f32),
                pltpu.VMEM((rows, cols), bf16),
                pltpu.VMEM((rows, cols), f32),
                pltpu.VMEM((slots, 2, half, cols), bf16),
                pltpu.VMEM((slots, 2, half, cols), bf16),
                pltpu.VMEM((2, half, cols), bf16),
                pltpu.VMEM((2, half, cols), bf16),
                pltpu.VMEM((2, half, cols), f32),
                pltpu.VMEM((2, 2, half // 2, cols), f32),
                pltpu.VMEM((2, 2, half // 2, cols), f32),
                pltpu.VMEM((3, 2, half // 2, cols), bf16),
                pltpu.VMEM((2, 4, half // 2, cols), bf16),
                pltpu.VMEM((layers, rows, cols), bf16),
                dma((layers * 4, dp_count - 1)), dma((layers * 4, dp_count - 1)),
                dma((dp_count, 4)), dma((dp_count, 4)),
                dma((layers,)), dma((layers + 2,)),
                dma((dp_count - 1,)), dma((dp_count - 1,)),
                dma((layers, dp_count - 1)), dma((layers, dp_count - 1)),
                dma((slots, 2)), dma((slots, 2)),
                dma((2,)), dma((2,)),
                dma((2, dp_count, 4)), dma((2, dp_count, 4)),
                dma((2,)), dma((2,)),
                dma((2, 3)), dma((2, 3)),
                dma((1,)), dma((1,)),
                dma((2,)), dma((2,)),
            ],
            compiler_params=pltpu.CompilerParams(
                collective_id=0, has_side_effects=True, vmem_limit_bytes=56 * 2**20
            ),
            cost_estimate=pl.CostEstimate(
                flops=12 * layers * rows * width * cols, bytes_accessed=2**23, transcendentals=0
            ),
        )(states, weights, guess_points, cotangent)

        def per_layer(*shape):
            return pl.BlockSpec((1, *shape), lambda layer: (layer, 0, 0))

        grads, adjoint = pl.pallas_call(
            weight_gradients,
            grid=(layers,),
            out_shape=(
                jax.ShapeDtypeStruct((layers, blk, cols), f32),
                jax.ShapeDtypeStruct((layers, rows, cols), bf16),
            ),
            in_specs=[per_layer(all_rows, blk), per_layer(all_rows, cols), per_layer(rows, cols)],
            out_specs=(per_layer(blk, cols), per_layer(rows, cols)),
            compiler_params=pltpu.CompilerParams(vmem_limit_bytes=60 * 2**20),
        )(inputs, scaled, adjoint)
        return adjoint, grads

    return jax.shard_map(
        body,
        mesh=mesh,
        in_specs=(
            P("layer", "dp", None),
            P("layer", "dp", "mp"),
            P("layer", "dp", None),
            P("dp", None),
        ),
        out_specs=(P("layer", "dp", "mp"), P("layer", "dp", "mp")),
        check_vma=False,
    )
```

```python
import functools

import jax
import jax.numpy as jnp
from jax import lax
from jax.experimental import pallas as pl
from jax.experimental.pallas import tpu as pltpu
from jax.sharding import PartitionSpec as P

step_size = 0.1
f32, bf16 = jnp.float32, jnp.bfloat16
MESH = pl.DeviceIdType.MESH


def back_product(scaled_rows, turned_block):
    return jnp.dot(scaled_rows, turned_block, preferred_element_type=f32)


def back_product_raw(scaled_rows, weight_block):
    return lax.dot_general(
        scaled_rows, weight_block, (((1,), (1,)), ((), ())), preferred_element_type=f32
    )


def slope_of(inputs, weight_block):
    tangent = jnp.tanh(jnp.dot(inputs, weight_block, preferred_element_type=f32))
    return 1.0 - tangent * tangent


def cycle(
    slab_count, dp_count, layers,
    states_in, weights, guess, cotangent, adjoint, sg, stg,
    states, gw, cw, wt, npt, slopes, cslopes, vbuf, sbuf, terminal,
    exs, exr, r0s, r0r, resid, pair_slopes, pair_resid, errs, spread_errs, sown,
    wsend, wrecv, csend, crecv, lsem, osem, ssend, srecv, gsend, grecv,
    xsend, xrecv, rsend, rrecv, ksend, krecv, psend, precv, qsend, qrecv, nsend, nrecv, hsend, hrecv,
):
    slab, mine, j = lax.axis_index("layer"), lax.axis_index("dp"), lax.axis_index("mp")
    o = 1 - j
    rows, width = states.shape[1], states.shape[2]
    blk, cols = weights.shape[1], weights.shape[2]
    half = rows // 2
    peers = range(1, dp_count)
    to_peer = [lax.rem(mine + d, dp_count) for d in peers]
    from_peer = [lax.rem(mine + dp_count - d, dp_count) for d in peers]
    not_top, not_low = slab < slab_count - 1, slab > 0
    core = lax.rem(slab, 2)
    sibling = slab + 1 - 2 * core
    pair_not_top, pair_not_low = slab < slab_count - 2, slab > 1
    quarter = half // 2
    keep = pl.ds(pl.multiple_of(core * quarter, quarter), quarter)
    give = pl.ds(pl.multiple_of((1 - core) * quarter, quarter), quarter)
    own_in = pl.ds(pl.multiple_of(mine * blk, blk), blk)
    own_rows = pl.ds(pl.multiple_of(mine * rows, rows), rows)
    half_j = pl.ds(pl.multiple_of(j * half, half), half)
    half_o = pl.ds(pl.multiple_of(o * half, half), half)
    cols_j = pl.ds(pl.multiple_of(j * cols, cols), cols)
    cols_o = pl.ds(pl.multiple_of(o * cols, cols), cols)

    def remote(src, dst, send, recv, device):
        return pltpu.make_async_remote_copy(
            src_ref=src, dst_ref=dst, send_sem=send, recv_sem=recv,
            device_id=device, device_id_type=MESH,
        )

    barrier = pltpu.get_barrier_semaphore()

    def greet(device):
        pl.semaphore_signal(barrier, inc=1, device_id=device, device_id_type=MESH)

    for peer in to_peer:
        greet({"dp": peer})
    greet({"mp": o})
    greet({"layer": sibling})
    greet({"layer": sibling, "mp": o})

    @pl.when(pair_not_top)
    def _():
        greet({"layer": slab + 2})

    @pl.when(pair_not_low)
    def _():
        greet({"layer": slab - 2})

    @pl.when(not_top)
    def _():
        greet({"layer": slab + 1})

    @pl.when(not_low)
    def _():
        greet({"layer": slab - 1})

    greeted = dp_count + 2
    for there in (not_top, not_low, pair_not_top, pair_not_low):
        greeted = greeted + there.astype(jnp.int32)
    pl.semaphore_wait(barrier, greeted)

    states_copy = pltpu.make_async_copy(states_in, states, osem.at[0])
    states_copy.start()

    def home(layer):
        return cw.at[core, j] if layer == 0 else gw.at[layer - 1]

    partner, twin = {"mp": o}, {"layer": sibling}
    point_copy = remote(guess.at[0, :, cols_j], npt, nsend.at[0], nrecv.at[0], {"layer": slab - 1})

    @pl.when(not_low)
    def _():
        point_copy.start()

    w_copies, local_copies = {}, {}
    pieces = 4
    piece = blk // pieces

    def piece_of(owner, n):
        return pl.ds(pl.multiple_of(owner * blk + n * piece, piece), piece)

    c_copies = [remote(weights.at[0], cw.at[core, j, own_in], csend.at[0, 0], crecv.at[0, 0], partner)]
    c_copies[0].start()
    c_blocks = [own_in]
    twin_copies = [
        remote(weights.at[0], cw.at[core, j, own_in], ksend.at[0, 0, 0], krecv.at[0, 0, 0], twin)
    ]
    twin_copies[0].start()
    order = range(layers - 1, -1, -1)
    stream = [(layer, n) for layer in order for n in range(pieces)]
    for layer, n in stream:
        for d in peers:
            w_copies[layer, n, d] = remote(
                weights.at[layer, n * piece:(n + 1) * piece],
                home(layer).at[piece_of(mine, n)],
                wsend.at[layer * pieces + n, d - 1], wrecv.at[layer * pieces + n, d - 1],
                {"dp": to_peer[d - 1]},
            )

    def start_piece(index):
        if index < len(stream):
            for d in peers:
                w_copies[(*stream[index], d)].start()

    def receive_piece(layer, n):
        for d in peers:
            w_copies[layer, n, d].wait_recv()
        start_piece(stream.index((layer, n)) + window)

    window = 5
    for index in range(window):
        start_piece(index)
    for layer in order:
        local_copies[layer] = pltpu.make_async_copy(
            weights.at[layer], home(layer).at[own_in], lsem.at[layer]
        )
        local_copies[layer].start()

    @pl.when(not_top)
    def _():
        point_copy.wait_recv()
        terminal[...] = npt[...].astype(f32)

    @pl.when(jnp.logical_not(not_top))
    def _():
        terminal[...] = cotangent[:, cols_j].astype(f32)

    pending = []
    span = [slice(0, half), slice(half, 2 * half)]

    def fine_half(slot, h, layer, scaled_rows):
        w = wt.at[layer - 1]
        exs[slot, h] = (step_size * back_product(scaled_rows, w[:, cols_o])).astype(bf16)
        copy = remote(
            exs.at[slot, h], exr.at[slot, h], xsend.at[slot, h], xrecv.at[slot, h], partner
        )
        copy.start()
        pending.append(copy)
        return copy, step_size * back_product(scaled_rows, w[:, cols_j])

    def arrived(value, copy, slot, h):
        if copy is None:
            return value
        copy.wait_recv()
        return value + exr[slot, h].astype(f32)

    v = [terminal[span[h], :] for h in range(2)]
    flying = [None, None]
    states_copy.wait()
    for slot, layer in enumerate(range(layers - 1, 0, -1)):
        local_copies[layer].wait()
        for n in range(pieces):
            receive_piece(layer, n)
        wt[layer - 1] = gw[layer - 1].T
        slopes[layer] = slope_of(states[layer], gw[layer - 1])
        for h in range(2):
            v[h] = arrived(v[h], flying[h], slot - 1, h)
            scaled_rows = (v[h] * slopes[layer, span[h], :]).astype(bf16)
            flying[h], term = fine_half(slot, h, layer, scaled_rows)
            v[h] = v[h] + term
    local_copies[0].wait()
    for n in range(pieces):
        receive_piece(0, n)
        for d in peers:
            c_blocks.append(piece_of(from_peer[d - 1], n))
            block = cw.at[core, j, c_blocks[-1]]
            c_copies.append(remote(block, block, csend.at[d, n], crecv.at[d, n], partner))
            c_copies[-1].start()
            twin_copies.append(remote(block, block, ksend.at[0, d, n], krecv.at[0, d, n], twin))
            twin_copies[-1].start()
    slopes[0] = slope_of(states[0], cw[core, j])
    for h in range(2):
        v[h] = arrived(v[h], flying[h], layers - 2, h)
        vbuf[span[h], :] = v[h]
        sbuf[span[h], :] = (v[h] * slopes[0, span[h], :]).astype(bf16)
    r0_copies = []
    s_far = sbuf[half_o, :]
    for c in range(2):
        far = step_size * back_product_raw(s_far, cw[core, j, c * cols:(c + 1) * cols, :])
        r0s[c] = (far + jnp.where(j == c, vbuf[half_o, :], 0.0)).astype(bf16)
        r0_copies.append(remote(r0s.at[c], r0r.at[c], rsend.at[c], rrecv.at[c], partner))
        r0_copies[c].start()
    pending += r0_copies

    s_copies = []
    for d in peers:
        block = pl.ds(pl.multiple_of(to_peer[d - 1] * blk, blk), blk)
        s_copies.append(
            remote(states_in.at[:, :, block], stg.at[:, own_rows, :], ssend.at[d - 1],
                   srecv.at[d - 1], {"dp": to_peer[d - 1]})
        )
        s_copies[-1].start()

    own_states = pltpu.make_async_copy(
        states_in.at[:, :, own_in], stg.at[:, own_rows, :], osem.at[1]
    )
    own_states.start()

    s_near = sbuf[half_j, :]
    for c in range(2):
        near = step_size * back_product_raw(s_near, cw[core, j, c * cols:(c + 1) * cols, :])
        near = near + jnp.where(j == c, vbuf[half_j, :], 0.0)
        resid[c] = near - guess[0, half_j, c * cols:(c + 1) * cols].astype(f32)
    for c in range(2):
        r0_copies[c].wait_recv()
        resid[c] = resid[c] + r0r[c].astype(f32)
    pair_resid[core] = resid[:, keep, :]
    twin_copies.append(
        remote(resid.at[:, give], pair_resid.at[core], psend.at[0], precv.at[0], twin)
    )
    twin_copies[-1].start()
    for n, (c_copy, block) in enumerate(zip(c_copies, c_blocks)):
        c_copy.wait_recv()
        d, m = (0, 0) if n == 0 else (1 + (n - 1) % (dp_count - 1), (n - 1) // (dp_count - 1))
        part = cw.at[core, o, block]
        twin_copies.append(remote(part, part, ksend.at[1, d, m], krecv.at[1, d, m], twin))
        twin_copies[-1].start()
    cslopes[j] = slopes[0, half_j, :]
    cslopes[o] = slope_of(states[0, half_j, :], cw[core, o])
    pair_slopes[core] = cslopes[:, keep, :]
    twin_copies.append(
        remote(cslopes.at[:, give], pair_slopes.at[core], psend.at[1], precv.at[1], twin)
    )
    twin_copies[-1].start()
    for copy in twin_copies:
        copy.wait_recv()

    chain = [
        remote(errs.at[2, n], errs.at[0, n], hsend.at[n], hrecv.at[n], {"layer": slab - 2})
        for n in range(2)
    ]

    def coarse_step(parity, start, incoming=None, outgoing=None):
        carried, products = [], [0.0, 0.0]
        for c in range(2):
            if incoming is not None:
                incoming[c].wait_recv()
            carried.append(errs[start, c].astype(f32))
            scaled_rows = (carried[c] * pair_slopes[parity, c]).astype(bf16)
            for n in range(2):
                block = cw[parity, c, n * cols:(n + 1) * cols, :]
                products[n] = products[n] + back_product_raw(scaled_rows, block)
                if c == 1:
                    total = carried[n] + layers * step_size * products[n] + pair_resid[parity, n]
                    errs[start + 1, n] = total.astype(bf16)
                    if outgoing is not None:

                        @pl.when(pair_not_low)
                        def _():
                            outgoing[n].start()

    @pl.when(jnp.logical_not(pair_not_top))
    def _():
        errs[0] = jnp.zeros(errs.shape[1:], bf16)
        for n in range(2):
            errs[1, n] = pair_resid[1, n].astype(bf16)

    @pl.when(pair_not_top)
    def _():
        coarse_step(1, 0, incoming=chain)

    place = 2 * j + core

    def scatter(kind):
        spread_errs[kind, place] = errs[1 - core + kind, j]
        copies = []
        for n, (index, c, device) in enumerate((
            (core + kind, j, twin),
            (1 - core + kind, o, partner),
            (core + kind, o, {"layer": sibling, "mp": o}),
        )):
            copies.append(
                remote(errs.at[index, c], spread_errs.at[kind, place], qsend.at[kind, n],
                       qrecv.at[kind, n], device)
            )
            copies[-1].start()
        return copies

    @pl.when(pair_not_low)
    def _():
        coarse_step(0, 1, outgoing=chain)

    in_copies = scatter(0)
    early = pending + c_copies + twin_copies + list(w_copies.values())
    pending = list(in_copies)

    for copy in in_copies:
        copy.wait_recv()
    v = [
        terminal[span[h], :]
        + jnp.concatenate([spread_errs[0, 2 * h + t].astype(f32) for t in range(2)], 0)
        for h in range(2)
    ]
    flying = [None, None]
    g_copies = {}

    own_scaled = []

    def spread(layer):
        for d in peers:
            g_copies[layer, d] = remote(
                sown.at[layer], sg.at[layer, own_rows],
                gsend.at[layer, d - 1], grecv.at[layer, d - 1], {"dp": to_peer[d - 1]},
            )
            g_copies[layer, d].start()
        own_scaled.append(
            pltpu.make_async_copy(sown.at[layer], sg.at[layer, own_rows], osem.at[2 + layer])
        )
        own_scaled[-1].start()

    for layer in range(layers - 1, -1, -1):
        slot = layers - 1 + (layers - 1 - layer)
        for h in range(2):
            v[h] = arrived(v[h], flying[h], slot - 1, h)
            scaled_rows = (v[h] * slopes[layer, span[h], :]).astype(bf16)
            sown[layer, span[h], :] = scaled_rows
            if layer < layers - 1:
                adjoint[layer + 1, span[h], :] = v[h].astype(bf16)
            if layer:
                flying[h], term = fine_half(slot, h, layer, scaled_rows)
                v[h] = v[h] + term
        spread(layer)
        if layer == layers - 1:
            for copy in early[:len(early) // 2]:
                copy.wait_send()
        if layer == max(layers - 2, 1):
            for copy in early[len(early) // 2:]:
                copy.wait_send()
        if layer == 1:

            @pl.when(jnp.logical_not(pair_not_low))
            def _():
                coarse_step(0, 1)

            own_copies = scatter(1)
            pending += own_copies
    for copy in own_copies:
        copy.wait_recv()
    for q in range(4):
        lines = slice(q * quarter, (q + 1) * quarter)
        own = guess[0, lines, cols_j].astype(f32) + spread_errs[1, q].astype(f32)
        adjoint[0, lines, :] = own.astype(bf16)
    for copy in s_copies + list(g_copies.values()):
        copy.wait_recv()
    for copy in own_scaled + [own_states]:
        copy.wait()
    for copy in pending + s_copies + list(g_copies.values()):
        copy.wait_send()

    @pl.when(not_low)
    def _():
        point_copy.wait_send()

    @pl.when(pair_not_low)
    def _():
        for n in range(2):
            chain[n].wait_send()


def weight_gradients(
    layers, inputs, scaled, adjoint_in, grads, adjoint, inputs_buf, scaled_buf, grads_buf, sems
):
    order = range(layers - 1, -1, -1)
    fetches = {}
    for layer in order:
        fetches[layer] = (
            pltpu.make_async_copy(inputs.at[layer], inputs_buf.at[layer], sems.at[0, layer]),
            pltpu.make_async_copy(scaled.at[layer], scaled_buf.at[layer], sems.at[1, layer]),
        )
        for copy in fetches[layer]:
            copy.start()
    stores = [pltpu.make_async_copy(adjoint_in, adjoint, sems.at[3, 0])]
    stores[0].start()
    for layer in order:
        for copy in fetches[layer]:
            copy.wait()
        product = lax.dot_general(
            inputs_buf[layer], scaled_buf[layer], (((0,), (0,)), ((), ())),
            preferred_element_type=f32,
        )
        grads_buf[layer] = step_size * product
        stores.append(
            pltpu.make_async_copy(grads_buf.at[layer], grads.at[layer], sems.at[2, layer])
        )
        stores[-1].start()
    for copy in stores:
        copy.wait()


def solution(mesh):
    slab_count, dp_count, mp_count = (mesh.shape[a] for a in ("layer", "dp", "mp"))
    assert mp_count == 2

    def body(states, weights, guess_points, cotangent):
        layers, rows, width = states.shape
        blk, cols = weights.shape[1:]
        assert guess_points.shape[0] == 1
        half = rows // 2
        slots = 2 * (layers - 1)
        assert slab_count % 2 == 0 and layers > 1 and blk % 64 == 0
        all_rows = rows * dp_count
        dma = pltpu.SemaphoreType.DMA
        vmem = pl.BlockSpec(memory_space=pltpu.VMEM)
        anywhere = pl.BlockSpec(memory_space=pl.ANY)
        adjoint, scaled, inputs = pl.pallas_call(
            functools.partial(cycle, slab_count, dp_count, layers),
            out_shape=(
                jax.ShapeDtypeStruct((layers, rows, cols), bf16),
                jax.ShapeDtypeStruct((layers, all_rows, cols), bf16),
                jax.ShapeDtypeStruct((layers, all_rows, blk), bf16),
            ),
            in_specs=[anywhere, anywhere, vmem, vmem],
            out_specs=(vmem, anywhere, anywhere),
            scratch_shapes=[
                pltpu.VMEM((layers, rows, width), bf16),
                pltpu.VMEM((layers - 1, width, cols), bf16),
                pltpu.VMEM((2, 2, width, cols), bf16),
                pltpu.VMEM((layers - 1, cols, width), bf16),
                pltpu.VMEM((rows, cols), bf16),
                pltpu.VMEM((layers, rows, cols), f32),
                pltpu.VMEM((2, half, cols), f32),
                pltpu.VMEM((rows, cols), f32),
                pltpu.VMEM((rows, cols), bf16),
                pltpu.VMEM((rows, cols), f32),
                pltpu.VMEM((slots, 2, half, cols), bf16),
                pltpu.VMEM((slots, 2, half, cols), bf16),
                pltpu.VMEM((2, half, cols), bf16),
                pltpu.VMEM((2, half, cols), bf16),
                pltpu.VMEM((2, half, cols), f32),
                pltpu.VMEM((2, 2, half // 2, cols), f32),
                pltpu.VMEM((2, 2, half // 2, cols), f32),
                pltpu.VMEM((3, 2, half // 2, cols), bf16),
                pltpu.VMEM((2, 4, half // 2, cols), bf16),
                pltpu.VMEM((layers, rows, cols), bf16),
                dma((layers * 4, dp_count - 1)), dma((layers * 4, dp_count - 1)),
                dma((dp_count, 4)), dma((dp_count, 4)),
                dma((layers,)), dma((layers + 2,)),
                dma((dp_count - 1,)), dma((dp_count - 1,)),
                dma((layers, dp_count - 1)), dma((layers, dp_count - 1)),
                dma((slots, 2)), dma((slots, 2)),
                dma((2,)), dma((2,)),
                dma((2, dp_count, 4)), dma((2, dp_count, 4)),
                dma((2,)), dma((2,)),
                dma((2, 3)), dma((2, 3)),
                dma((1,)), dma((1,)),
                dma((2,)), dma((2,)),
            ],
            compiler_params=pltpu.CompilerParams(
                collective_id=0, has_side_effects=True, vmem_limit_bytes=56 * 2**20
            ),
            cost_estimate=pl.CostEstimate(
                flops=12 * layers * rows * width * cols, bytes_accessed=2**23, transcendentals=0
            ),
        )(states, weights, guess_points, cotangent)

        grads, adjoint = pl.pallas_call(
            functools.partial(weight_gradients, layers),
            out_shape=(
                jax.ShapeDtypeStruct((layers, blk, cols), f32),
                jax.ShapeDtypeStruct((layers, rows, cols), bf16),
            ),
            in_specs=[anywhere] * 3,
            out_specs=(anywhere, anywhere),
            scratch_shapes=[
                pltpu.VMEM((layers, all_rows, blk), bf16),
                pltpu.VMEM((layers, all_rows, cols), bf16),
                pltpu.VMEM((layers, blk, cols), f32),
                dma((4, layers)),
            ],
            compiler_params=pltpu.CompilerParams(vmem_limit_bytes=60 * 2**20),
        )(inputs, scaled, adjoint)
        return adjoint, grads

    return jax.shard_map(
        body,
        mesh=mesh,
        in_specs=(
            P("layer", "dp", None),
            P("layer", "dp", "mp"),
            P("layer", "dp", None),
            P("dp", None),
        ),
        out_specs=(P("layer", "dp", "mp"), P("layer", "dp", "mp")),
        check_vma=False,
    )
```

```python
import functools

import jax
import jax.numpy as jnp
from jax import lax
from jax.experimental import pallas as pl
from jax.experimental.pallas import tpu as pltpu
from jax.sharding import PartitionSpec as P

step_size = 0.1
f32, bf16 = jnp.float32, jnp.bfloat16
MESH = pl.DeviceIdType.MESH


def back_product(scaled_rows, turned_block):
    return jnp.dot(scaled_rows, turned_block, preferred_element_type=f32)


def back_product_raw(scaled_rows, weight_block):
    return lax.dot_general(
        scaled_rows, weight_block, (((1,), (1,)), ((), ())), preferred_element_type=f32
    )


def slope_of(inputs, weight_block):
    tangent = jnp.tanh(jnp.dot(inputs, weight_block, preferred_element_type=f32))
    return 1.0 - tangent * tangent


def cycle(
    slab_count, dp_count, layers,
    states_in, weights, guess, cotangent, adjoint, sg, stg,
    states, gw, cw, wt, npt, slopes, cslopes, vbuf, sbuf, terminal,
    exs, exr, r0s, r0r, resid, pair_slopes, pair_resid, errs, spread_errs, sown,
    wsend, wrecv, csend, crecv, lsem, osem, ssend, srecv, gsend, grecv,
    xsend, xrecv, rsend, rrecv, ksend, krecv, psend, precv, qsend, qrecv, nsend, nrecv, hsend, hrecv,
):
    slab, mine, j = lax.axis_index("layer"), lax.axis_index("dp"), lax.axis_index("mp")
    o = 1 - j
    rows, width = states.shape[1], states.shape[2]
    blk, cols = weights.shape[1], weights.shape[2]
    half = rows // 2
    peers = range(1, dp_count)
    to_peer = [lax.rem(mine + d, dp_count) for d in peers]
    from_peer = [lax.rem(mine + dp_count - d, dp_count) for d in peers]
    not_top, not_low = slab < slab_count - 1, slab > 0
    core = lax.rem(slab, 2)
    sibling = slab + 1 - 2 * core
    pair_not_top, pair_not_low = slab < slab_count - 2, slab > 1
    quarter = half // 2
    keep = pl.ds(pl.multiple_of(core * quarter, quarter), quarter)
    give = pl.ds(pl.multiple_of((1 - core) * quarter, quarter), quarter)
    own_in = pl.ds(pl.multiple_of(mine * blk, blk), blk)
    own_rows = pl.ds(pl.multiple_of(mine * rows, rows), rows)
    half_j = pl.ds(pl.multiple_of(j * half, half), half)
    half_o = pl.ds(pl.multiple_of(o * half, half), half)
    cols_j = pl.ds(pl.multiple_of(j * cols, cols), cols)
    cols_o = pl.ds(pl.multiple_of(o * cols, cols), cols)

    def remote(src, dst, send, recv, device):
        return pltpu.make_async_remote_copy(
            src_ref=src, dst_ref=dst, send_sem=send, recv_sem=recv,
            device_id=device, device_id_type=MESH,
        )

    barrier = pltpu.get_barrier_semaphore()

    def greet(device):
        pl.semaphore_signal(barrier, inc=1, device_id=device, device_id_type=MESH)

    for peer in to_peer:
        greet({"dp": peer})
    greet({"mp": o})
    greet({"layer": sibling})
    greet({"layer": sibling, "mp": o})

    @pl.when(pair_not_top)
    def _():
        greet({"layer": slab + 2})

    @pl.when(pair_not_low)
    def _():
        greet({"layer": slab - 2})

    @pl.when(not_top)
    def _():
        greet({"layer": slab + 1})

    @pl.when(not_low)
    def _():
        greet({"layer": slab - 1})

    greeted = dp_count + 2
    for there in (not_top, not_low, pair_not_top, pair_not_low):
        greeted = greeted + there.astype(jnp.int32)
    pl.semaphore_wait(barrier, greeted)

    states_copy = pltpu.make_async_copy(states_in, states, osem.at[0])
    states_copy.start()

    def home(layer):
        return cw.at[core, j] if layer == 0 else gw.at[layer - 1]

    partner, twin = {"mp": o}, {"layer": sibling}
    point_copy = remote(guess.at[0, :, cols_j], npt, nsend.at[0], nrecv.at[0], {"layer": slab - 1})

    @pl.when(not_low)
    def _():
        point_copy.start()

    w_copies, local_copies = {}, {}
    pieces = 4
    piece = blk // pieces

    def piece_of(owner, n):
        return pl.ds(pl.multiple_of(owner * blk + n * piece, piece), piece)

    c_copies = [remote(weights.at[0], cw.at[core, j, own_in], csend.at[0, 0], crecv.at[0, 0], partner)]
    c_copies[0].start()
    c_blocks = [own_in]
    twin_copies = [
        remote(weights.at[0], cw.at[core, j, own_in], ksend.at[0, 0, 0], krecv.at[0, 0, 0], twin)
    ]
    twin_copies[0].start()
    order = range(layers - 1, -1, -1)
    stream = [(layer, n) for layer in order for n in range(pieces)]
    for layer, n in stream:
        for d in peers:
            w_copies[layer, n, d] = remote(
                weights.at[layer, n * piece:(n + 1) * piece],
                home(layer).at[piece_of(mine, n)],
                wsend.at[layer * pieces + n, d - 1], wrecv.at[layer * pieces + n, d - 1],
                {"dp": to_peer[d - 1]},
            )

    def start_piece(index):
        if index < len(stream):
            for d in peers:
                w_copies[(*stream[index], d)].start()

    def receive_piece(layer, n):
        for d in peers:
            w_copies[layer, n, d].wait_recv()
        start_piece(stream.index((layer, n)) + window)

    window = 5
    for index in range(window):
        start_piece(index)
    for layer in order:
        local_copies[layer] = pltpu.make_async_copy(
            weights.at[layer], home(layer).at[own_in], lsem.at[layer]
        )
        local_copies[layer].start()

    @pl.when(not_top)
    def _():
        point_copy.wait_recv()
        terminal[...] = npt[...].astype(f32)

    @pl.when(jnp.logical_not(not_top))
    def _():
        terminal[...] = cotangent[:, cols_j].astype(f32)

    pending = []
    span = [slice(0, half), slice(half, 2 * half)]

    def fine_half(slot, h, layer, scaled_rows):
        w = wt.at[layer - 1]
        exs[slot, h] = (step_size * back_product(scaled_rows, w[:, cols_o])).astype(bf16)
        copy = remote(
            exs.at[slot, h], exr.at[slot, h], xsend.at[slot, h], xrecv.at[slot, h], partner
        )
        copy.start()
        pending.append(copy)
        return copy, step_size * back_product(scaled_rows, w[:, cols_j])

    def arrived(value, copy, slot, h):
        if copy is None:
            return value
        copy.wait_recv()
        return value + exr[slot, h].astype(f32)

    v = [terminal[span[h], :] for h in range(2)]
    flying = [None, None]
    states_copy.wait()
    for slot, layer in enumerate(range(layers - 1, 0, -1)):
        local_copies[layer].wait()
        for n in range(pieces):
            receive_piece(layer, n)
        wt[layer - 1] = gw[layer - 1].T
        slopes[layer] = slope_of(states[layer], gw[layer - 1])
        for h in range(2):
            v[h] = arrived(v[h], flying[h], slot - 1, h)
            scaled_rows = (v[h] * slopes[layer, span[h], :]).astype(bf16)
            flying[h], term = fine_half(slot, h, layer, scaled_rows)
            v[h] = v[h] + term
    local_copies[0].wait()
    for n in range(pieces):
        receive_piece(0, n)
        for d in peers:
            c_blocks.append(piece_of(from_peer[d - 1], n))
            block = cw.at[core, j, c_blocks[-1]]
            c_copies.append(remote(block, block, csend.at[d, n], crecv.at[d, n], partner))
            c_copies[-1].start()
            twin_copies.append(remote(block, block, ksend.at[0, d, n], krecv.at[0, d, n], twin))
            twin_copies[-1].start()
    slopes[0] = slope_of(states[0], cw[core, j])
    for h in range(2):
        v[h] = arrived(v[h], flying[h], layers - 2, h)
        vbuf[span[h], :] = v[h]
        sbuf[span[h], :] = (v[h] * slopes[0, span[h], :]).astype(bf16)
    r0_copies = []
    s_far = sbuf[half_o, :]
    for c in range(2):
        far = step_size * back_product_raw(s_far, cw[core, j, c * cols:(c + 1) * cols, :])
        r0s[c] = (far + jnp.where(j == c, vbuf[half_o, :], 0.0)).astype(bf16)
        r0_copies.append(remote(r0s.at[c], r0r.at[c], rsend.at[c], rrecv.at[c], partner))
        r0_copies[c].start()
    pending += r0_copies

    s_copies = []
    for d in peers:
        block = pl.ds(pl.multiple_of(to_peer[d - 1] * blk, blk), blk)
        s_copies.append(
            remote(states.at[:, :, block], stg.at[:, own_rows, :], ssend.at[d - 1],
                   srecv.at[d - 1], {"dp": to_peer[d - 1]})
        )
        s_copies[-1].start()

    own_states = pltpu.make_async_copy(
        states.at[:, :, own_in], stg.at[:, own_rows, :], osem.at[1]
    )
    own_states.start()

    s_near = sbuf[half_j, :]
    for c in range(2):
        near = step_size * back_product_raw(s_near, cw[core, j, c * cols:(c + 1) * cols, :])
        near = near + jnp.where(j == c, vbuf[half_j, :], 0.0)
        resid[c] = near - guess[0, half_j, c * cols:(c + 1) * cols].astype(f32)
    for c in range(2):
        r0_copies[c].wait_recv()
        resid[c] = resid[c] + r0r[c].astype(f32)
    pair_resid[core] = resid[:, keep, :]
    twin_copies.append(
        remote(resid.at[:, give], pair_resid.at[core], psend.at[0], precv.at[0], twin)
    )
    twin_copies[-1].start()
    for n, (c_copy, block) in enumerate(zip(c_copies, c_blocks)):
        c_copy.wait_recv()
        d, m = (0, 0) if n == 0 else (1 + (n - 1) % (dp_count - 1), (n - 1) // (dp_count - 1))
        part = cw.at[core, o, block]
        twin_copies.append(remote(part, part, ksend.at[1, d, m], krecv.at[1, d, m], twin))
        twin_copies[-1].start()
    cslopes[j] = slopes[0, half_j, :]
    cslopes[o] = slope_of(states[0, half_j, :], cw[core, o])
    pair_slopes[core] = cslopes[:, keep, :]
    twin_copies.append(
        remote(cslopes.at[:, give], pair_slopes.at[core], psend.at[1], precv.at[1], twin)
    )
    twin_copies[-1].start()
    for copy in twin_copies:
        copy.wait_recv()

    chain = [
        remote(errs.at[2, n], errs.at[0, n], hsend.at[n], hrecv.at[n], {"layer": slab - 2})
        for n in range(2)
    ]

    def coarse_step(parity, start, incoming=None, outgoing=None):
        carried, products = [], [0.0, 0.0]
        for c in range(2):
            if incoming is not None:
                incoming[c].wait_recv()
            carried.append(errs[start, c].astype(f32))
            scaled_rows = (carried[c] * pair_slopes[parity, c]).astype(bf16)
            for n in range(2):
                block = cw[parity, c, n * cols:(n + 1) * cols, :]
                products[n] = products[n] + back_product_raw(scaled_rows, block)
                if c == 1:
                    total = carried[n] + layers * step_size * products[n] + pair_resid[parity, n]
                    errs[start + 1, n] = total.astype(bf16)
                    if outgoing is not None:

                        @pl.when(pair_not_low)
                        def _():
                            outgoing[n].start()

    @pl.when(jnp.logical_not(pair_not_top))
    def _():
        errs[0] = jnp.zeros(errs.shape[1:], bf16)
        for n in range(2):
            errs[1, n] = pair_resid[1, n].astype(bf16)

    @pl.when(pair_not_top)
    def _():
        coarse_step(1, 0, incoming=chain)

    place = 2 * j + core

    def scatter(kind):
        spread_errs[kind, place] = errs[1 - core + kind, j]
        copies = []
        for n, (index, c, device) in enumerate((
            (core + kind, j, twin),
            (1 - core + kind, o, partner),
            (core + kind, o, {"layer": sibling, "mp": o}),
        )):
            copies.append(
                remote(errs.at[index, c], spread_errs.at[kind, place], qsend.at[kind, n],
                       qrecv.at[kind, n], device)
            )
            copies[-1].start()
        return copies

    @pl.when(pair_not_low)
    def _():
        coarse_step(0, 1, outgoing=chain)

    in_copies = scatter(0)
    early = pending + c_copies + twin_copies + list(w_copies.values())
    pending = list(in_copies)

    for copy in in_copies:
        copy.wait_recv()
    v = [
        terminal[span[h], :]
        + jnp.concatenate([spread_errs[0, 2 * h + t].astype(f32) for t in range(2)], 0)
        for h in range(2)
    ]
    flying = [None, None]
    g_copies = {}

    own_scaled = []

    def spread(layer):
        for d in peers:
            g_copies[layer, d] = remote(
                sown.at[layer], sg.at[layer, own_rows],
                gsend.at[layer, d - 1], grecv.at[layer, d - 1], {"dp": to_peer[d - 1]},
            )
            g_copies[layer, d].start()
        own_scaled.append(
            pltpu.make_async_copy(sown.at[layer], sg.at[layer, own_rows], osem.at[2 + layer])
        )
        own_scaled[-1].start()

    for layer in range(layers - 1, -1, -1):
        slot = layers - 1 + (layers - 1 - layer)
        for h in range(2):
            v[h] = arrived(v[h], flying[h], slot - 1, h)
            scaled_rows = (v[h] * slopes[layer, span[h], :]).astype(bf16)
            sown[layer, span[h], :] = scaled_rows
            if layer < layers - 1:
                adjoint[layer + 1, span[h], :] = v[h].astype(bf16)
            if layer:
                flying[h], term = fine_half(slot, h, layer, scaled_rows)
                v[h] = v[h] + term
        spread(layer)
        if layer == layers - 1:
            for copy in early[:len(early) // 2]:
                copy.wait_send()
        if layer == max(layers - 2, 1):
            for copy in early[len(early) // 2:]:
                copy.wait_send()
        if layer == 1:

            @pl.when(jnp.logical_not(pair_not_low))
            def _():
                coarse_step(0, 1)

            own_copies = scatter(1)
            pending += own_copies
    for copy in own_copies:
        copy.wait_recv()
    for q in range(4):
        lines = slice(q * quarter, (q + 1) * quarter)
        own = guess[0, lines, cols_j].astype(f32) + spread_errs[1, q].astype(f32)
        adjoint[0, lines, :] = own.astype(bf16)
    for copy in s_copies + list(g_copies.values()):
        copy.wait_recv()
    for copy in own_scaled + [own_states]:
        copy.wait()
    for copy in pending + s_copies + list(g_copies.values()):
        copy.wait_send()

    @pl.when(not_low)
    def _():
        point_copy.wait_send()

    @pl.when(pair_not_low)
    def _():
        for n in range(2):
            chain[n].wait_send()


def weight_gradients(
    layers, inputs, scaled, adjoint_in, grads, adjoint, inputs_buf, scaled_buf, grads_buf, sems
):
    order = range(layers - 1, -1, -1)
    fetches = {}
    for layer in order:
        fetches[layer] = (
            pltpu.make_async_copy(inputs.at[layer], inputs_buf.at[layer], sems.at[0, layer]),
            pltpu.make_async_copy(scaled.at[layer], scaled_buf.at[layer], sems.at[1, layer]),
        )
        for copy in fetches[layer]:
            copy.start()
    stores = []
    adjoint[...] = adjoint_in[...]
    for layer in order:
        for copy in fetches[layer]:
            copy.wait()
        product = lax.dot_general(
            inputs_buf[layer], scaled_buf[layer], (((0,), (0,)), ((), ())),
            preferred_element_type=f32,
        )
        grads_buf[layer] = step_size * product
        stores.append(
            pltpu.make_async_copy(grads_buf.at[layer], grads.at[layer], sems.at[2, layer])
        )
        stores[-1].start()
    for copy in stores:
        copy.wait()


def solution(mesh):
    slab_count, dp_count, mp_count = (mesh.shape[a] for a in ("layer", "dp", "mp"))
    assert mp_count == 2

    def body(states, weights, guess_points, cotangent):
        layers, rows, width = states.shape
        blk, cols = weights.shape[1:]
        assert guess_points.shape[0] == 1
        half = rows // 2
        slots = 2 * (layers - 1)
        assert slab_count % 2 == 0 and layers > 1 and blk % 64 == 0
        all_rows = rows * dp_count
        dma = pltpu.SemaphoreType.DMA
        vmem = pl.BlockSpec(memory_space=pltpu.VMEM)
        anywhere = pl.BlockSpec(memory_space=pl.ANY)
        adjoint, scaled, inputs = pl.pallas_call(
            functools.partial(cycle, slab_count, dp_count, layers),
            out_shape=(
                jax.ShapeDtypeStruct((layers, rows, cols), bf16),
                jax.ShapeDtypeStruct((layers, all_rows, cols), bf16),
                jax.ShapeDtypeStruct((layers, all_rows, blk), bf16),
            ),
            in_specs=[anywhere, anywhere, vmem, vmem],
            out_specs=(vmem, anywhere, anywhere),
            scratch_shapes=[
                pltpu.VMEM((layers, rows, width), bf16),
                pltpu.VMEM((layers - 1, width, cols), bf16),
                pltpu.VMEM((2, 2, width, cols), bf16),
                pltpu.VMEM((layers - 1, cols, width), bf16),
                pltpu.VMEM((rows, cols), bf16),
                pltpu.VMEM((layers, rows, cols), f32),
                pltpu.VMEM((2, half, cols), f32),
                pltpu.VMEM((rows, cols), f32),
                pltpu.VMEM((rows, cols), bf16),
                pltpu.VMEM((rows, cols), f32),
                pltpu.VMEM((slots, 2, half, cols), bf16),
                pltpu.VMEM((slots, 2, half, cols), bf16),
                pltpu.VMEM((2, half, cols), bf16),
                pltpu.VMEM((2, half, cols), bf16),
                pltpu.VMEM((2, half, cols), f32),
                pltpu.VMEM((2, 2, half // 2, cols), f32),
                pltpu.VMEM((2, 2, half // 2, cols), f32),
                pltpu.VMEM((3, 2, half // 2, cols), bf16),
                pltpu.VMEM((2, 4, half // 2, cols), bf16),
                pltpu.VMEM((layers, rows, cols), bf16),
                dma((layers * 4, dp_count - 1)), dma((layers * 4, dp_count - 1)),
                dma((dp_count, 4)), dma((dp_count, 4)),
                dma((layers,)), dma((layers + 2,)),
                dma((dp_count - 1,)), dma((dp_count - 1,)),
                dma((layers, dp_count - 1)), dma((layers, dp_count - 1)),
                dma((slots, 2)), dma((slots, 2)),
                dma((2,)), dma((2,)),
                dma((2, dp_count, 4)), dma((2, dp_count, 4)),
                dma((2,)), dma((2,)),
                dma((2, 3)), dma((2, 3)),
                dma((1,)), dma((1,)),
                dma((2,)), dma((2,)),
            ],
            compiler_params=pltpu.CompilerParams(
                collective_id=0, has_side_effects=True, vmem_limit_bytes=56 * 2**20
            ),
            cost_estimate=pl.CostEstimate(
                flops=12 * layers * rows * width * cols, bytes_accessed=2**23, transcendentals=0
            ),
        )(states, weights, guess_points, cotangent)

        grads, adjoint = pl.pallas_call(
            functools.partial(weight_gradients, layers),
            out_shape=(
                jax.ShapeDtypeStruct((layers, blk, cols), f32),
                jax.ShapeDtypeStruct((layers, rows, cols), bf16),
            ),
            in_specs=[anywhere, anywhere, vmem],
            out_specs=(anywhere, vmem),
            scratch_shapes=[
                pltpu.VMEM((layers, all_rows, blk), bf16),
                pltpu.VMEM((layers, all_rows, cols), bf16),
                pltpu.VMEM((layers, blk, cols), f32),
                dma((3, layers)),
            ],
            compiler_params=pltpu.CompilerParams(vmem_limit_bytes=60 * 2**20),
        )(inputs, scaled, adjoint)
        return adjoint, grads

    return jax.shard_map(
        body,
        mesh=mesh,
        in_specs=(
            P("layer", "dp", None),
            P("layer", "dp", "mp"),
            P("layer", "dp", None),
            P("dp", None),
        ),
        out_specs=(P("layer", "dp", "mp"), P("layer", "dp", "mp")),
        check_vma=False,
    )
```
